256 devices in a mesh: dp: 64 (over z, x_lo, y), mp: 4 (over x_hi, core).
Axes of the slice: x: 4 (x_hi: 2, x_lo: 2; x = x_hi * 2 + x_lo), y: 4, z: 8, core: 2. Of those that a mesh axis runs over, the one named last changes fastest.
Arguments:
- hidden_t: bfloat16 [29568, 8192], P(None, 'dp'), may hold values from -6 to 6
- cotangent: bfloat16 [8192, 4096], P('dp', 'mp'), may hold values from -0.0625 to 0.0625
- momentum: float32 [29568, 4096], P('dp', 'mp'), may hold values from -6 to 6
- basis: float32 [4096, 512], P('mp', 'dp'), may hold values from -0.09375 to 0.09375
Outputs:
- new_momentum: float32 [29568, 4096], P('dp', 'mp')
- new_basis: float32 [4096, 512], P('mp', 'dp')
- direction: bfloat16 [29568, 4096], P('dp', 'mp')
The draws below stay inside these ranges and needn't reach their ends.
All inputs are finite; a program needn't handle non-finite values.
Results may differ from the reference program's by a relative error of at most 0.0015.
Values may be sent and summed in bfloat16 or wider, within the bound.
A program may use at most 320 MiB of HBM per device.

```python
import jax
import jax.numpy as jnp
from jax import lax

D = 4096
FF = 29568
RANK = 512
TOKENS = 8192


def shard_levels(stream_key, shape, shards, least, top_value):
    def one(position, parts):
        heights = jax.random.uniform(jax.random.fold_in(jax.random.fold_in(stream_key, 6), position), (parts,), jnp.float32, least / len(shards), top_value / len(shards))
        return jnp.repeat(jnp.exp(heights), shape[position] // parts).reshape((-1,) + (1,) * (len(shape) - position - 1))

    level = one(*shards[0])
    for cut in shards[1:]:
        level = level * one(*cut)
    return level


def normal_values(own_key, dims, scale, reach, split=(), held_as=jnp.bfloat16):
    result = scale * jax.random.normal(own_key, dims, jnp.float32)
    if split:
        result = result * shard_levels(own_key, dims, split, -0.22, 0.18)
    return jnp.clip(result, -reach, reach).astype(held_as)


def setup_inputs(seed: int = 0) -> dict:
    streams_of = jax.random.split(jax.random.key(seed), 5)
    hidden_t = normal_values(streams_of[0], (FF, TOKENS), 1.0, 6.0, ((1, 64),))
    cotangent = normal_values(streams_of[1], (TOKENS, D), TOKENS ** -0.5, 0.0625, ((0, 64), (1, 4)))
    momentum = normal_values(streams_of[2], (FF, D), 1.0, 6.0, ((0, 64), (1, 4)), jnp.float32)
    basis = normal_values(streams_of[3], (D, RANK), D ** -0.5, 0.09375, ((0, 4), (1, 64)), jnp.float32)
    return dict(hidden_t=hidden_t, cotangent=cotangent, momentum=momentum, basis=basis)


epsilon = 1e-06
momentum_rate = 0.95

def reference(hidden_t, cotangent, momentum, basis):
    highest = lax.Precision.HIGHEST
    gradient = jnp.dot(hidden_t.astype(jnp.float32), cotangent.astype(jnp.float32), preferred_element_type=jnp.float32)
    merged = momentum + gradient
    left_prod = jnp.dot(merged, basis, precision=highest)
    gram_sum = jnp.dot(left_prod.T, left_prod, precision=highest)
    factor = jnp.linalg.cholesky(gram_sum)
    orthonormal = jax.scipy.linalg.solve_triangular(factor, left_prod.T, lower=True).T
    right_full = jnp.dot(merged.T, orthonormal, precision=highest)
    new_momentum = merged - (1.0 - momentum_rate) * jnp.dot(orthonormal, right_full.T, precision=highest)
    squares = lax.optimization_barrier(jnp.sum(right_full * right_full, axis=0))
    new_basis = right_full / (jnp.sqrt(squares) + epsilon)
    direction_scale = (FF * D / RANK) ** 0.5
    direction = (direction_scale * jnp.dot(orthonormal, new_basis.T, precision=highest)).astype(jnp.bfloat16)
    return (new_momentum, new_basis, direction)
```

```python
import jax
import jax.numpy as jnp
from jax import lax
from jax.experimental import pallas as pl
from jax.experimental.pallas import tpu as pltpu
from jax.sharding import PartitionSpec as P

D = 4096
FF = 29568
RANK = 512

NY, NXL, NZ = 4, 2, 8

epsilon = 1e-06
momentum_rate = 0.95


def place():
    dp = lax.axis_index("dp")
    return dp // (NXL * NY), (dp // NY) % NXL, dp % NY


def dp_of(z, xl, y):
    return (z * NXL + xl) * NY + y


def greet(partners):
    barrier = pltpu.get_barrier_semaphore()
    for device in partners:
        pl.semaphore_signal(
            barrier, inc=1, device_id=device, device_id_type=pl.DeviceIdType.MESH
        )
    pl.semaphore_wait(barrier, len(partners))


def send(src, dst, send_sem, recv_sem, device):
    copy = pltpu.make_async_remote_copy(
        src_ref=src,
        dst_ref=dst,
        send_sem=send_sem,
        recv_sem=recv_sem,
        device_id=device,
        device_id_type=pl.DeviceIdType.MESH,
    )
    copy.start()
    return copy


def sum_kernel(in_ref, out_ref, buf_y, buf_x, buf_z, acc_y, acc_x, send_sems, recv_sems):
    z, xl, y = place()
    rows = in_ref.shape[0]
    ry, rx, rz = rows // NY, rows // (NY * NXL), rows // (NY * NXL * NZ)
    to_y = [{"dp": dp_of(z, xl, (y + k) % NY)} for k in range(1, NY)]
    to_x = {"dp": dp_of(z, 1 - xl, y)}
    to_z = [{"dp": dp_of((z + k) % NZ, xl, y)} for k in range(1, NZ)]
    greet(to_y + [to_x] + to_z)

    sem = iter(range(22))

    def start(src, dst, device):
        s = next(sem)
        return send(src, dst, send_sems.at[s], recv_sems.at[s], device)

    copies = [
        start(in_ref.at[pl.ds(((y + k) % NY) * ry, ry)], buf_y.at[k - 1], to_y[k - 1])
        for k in range(1, NY)
    ]
    acc_y[...] = in_ref[pl.ds(y * ry, ry), :]
    for copy in copies:
        copy.wait()
    acc_y[...] += buf_y[0] + buf_y[1] + buf_y[2]

    copy = start(acc_y.at[pl.ds((1 - xl) * rx, rx)], buf_x, to_x)
    copy.wait()
    acc_x[...] = acc_y[pl.ds(xl * rx, rx), :] + buf_x[...]

    copies = [
        start(acc_x.at[pl.ds(((z + k) % NZ) * rz, rz)], buf_z.at[k - 1], to_z[k - 1])
        for k in range(1, NZ)
    ]
    total = acc_x[pl.ds(z * rz, rz), :]
    for k in range(NZ - 1):
        copies[k].wait()
        total = total + buf_z[k]
    base = y * ry + xl * rx
    mine = out_ref.at[pl.ds(base + z * rz, rz)]
    out_ref[pl.ds(base + z * rz, rz), :] = total
    copies = [start(mine, mine, to_z[k]) for k in range(NZ - 1)]
    for copy in copies:
        copy.wait()
    mine = out_ref.at[pl.ds(base, rx)]
    start(mine, mine, to_x).wait()
    mine = out_ref.at[pl.ds(y * ry, ry)]
    copies = [start(mine, mine, to_y[k]) for k in range(NY - 1)]
    for copy in copies:
        copy.wait()


def sum_over_dp(x):
    rows, cols = x.shape
    f32 = jnp.float32
    return pl.pallas_call(
        sum_kernel,
        out_shape=jax.ShapeDtypeStruct(x.shape, f32),
        in_specs=[pl.BlockSpec(memory_space=pltpu.VMEM)],
        out_specs=pl.BlockSpec(memory_space=pltpu.VMEM),
        scratch_shapes=[
            pltpu.VMEM((NY - 1, rows // NY, cols), f32),
            pltpu.VMEM((rows // (NY * NXL), cols), f32),
            pltpu.VMEM((NZ - 1, rows // (NY * NXL * NZ), cols), f32),
            pltpu.VMEM((rows // NY, cols), f32),
            pltpu.VMEM((rows // (NY * NXL), cols), f32),
            pltpu.SemaphoreType.DMA((22,)),
            pltpu.SemaphoreType.DMA((22,)),
        ],
        compiler_params=pltpu.CompilerParams(
            collective_id=1, has_side_effects=True, vmem_limit_bytes=40 << 20
        ),
    )(x)


def per_device(hidden_t, cotangent, momentum, basis):
    highest = lax.Precision.HIGHEST
    row_block = lax.all_to_all(hidden_t, "dp", split_axis=0, concat_axis=1, tiled=True)
    gradient = jnp.dot(
        row_block,
        lax.all_gather(cotangent, "dp", axis=0, tiled=True),
        preferred_element_type=jnp.float32,
    )
    whole_basis = lax.all_gather(basis.T, "dp", axis=0, tiled=True).T
    merged = momentum + gradient
    left_prod = lax.psum(jnp.dot(merged, whole_basis, precision=highest), "mp")
    gram_part = jnp.dot(left_prod.T, left_prod, precision=highest)
    right_part = jnp.dot(merged.T, left_prod, precision=highest)
    sums = sum_over_dp(jnp.concatenate([right_part, gram_part], axis=0))
    gram_sum = sums[1024:]
    factor = jnp.linalg.cholesky(gram_sum)
    inverse = jax.scipy.linalg.solve_triangular(
        factor, jnp.eye(RANK, dtype=jnp.float32), lower=True
    )
    orthonormal = jnp.dot(left_prod, inverse.T, precision=highest)
    rank_share = basis.shape[1]
    right_full = jnp.dot(sums[:1024], inverse.T, precision=highest)
    squares = lax.psum(jnp.sum(right_full * right_full, axis=0), "mp")
    unit_cols = right_full / (jnp.sqrt(squares) + epsilon)
    new_basis = lax.dynamic_slice_in_dim(
        unit_cols, lax.axis_index("dp") * rank_share, rank_share, 1
    )
    new_momentum = merged - (1.0 - momentum_rate) * jnp.dot(
        orthonormal, right_full.T, precision=highest
    )
    direction_scale = (FF * D / RANK) ** 0.5
    direction = (direction_scale * jnp.dot(orthonormal, unit_cols.T, precision=highest)).astype(
        jnp.bfloat16
    )
    return (new_momentum, new_basis, direction)


def solution(mesh):
    in_specs = (P(None, "dp"), P("dp", "mp"), P("dp", "mp"), P("mp", "dp"))
    out_specs = (P("dp", "mp"), P("mp", "dp"), P("dp", "mp"))
    return jax.shard_map(
        per_device, mesh=mesh, in_specs=in_specs, out_specs=out_specs, check_vma=False
    )
```

```python
import jax
import jax.numpy as jnp
from jax import lax
from jax.experimental import pallas as pl
from jax.experimental.pallas import tpu as pltpu
from jax.sharding import PartitionSpec as P

D = 4096
FF = 29568
RANK = 512

NY, NXL, NZ = 4, 2, 8

epsilon = 1e-06
momentum_rate = 0.95


def place():
    dp = lax.axis_index("dp")
    return dp // (NXL * NY), (dp // NY) % NXL, dp % NY


def dp_of(z, xl, y):
    return (z * NXL + xl) * NY + y


def greet(partners):
    barrier = pltpu.get_barrier_semaphore()
    for device in partners:
        pl.semaphore_signal(
            barrier, inc=1, device_id=device, device_id_type=pl.DeviceIdType.MESH
        )
    pl.semaphore_wait(barrier, len(partners))


def send(src, dst, send_sem, recv_sem, device):
    copy = pltpu.make_async_remote_copy(
        src_ref=src,
        dst_ref=dst,
        send_sem=send_sem,
        recv_sem=recv_sem,
        device_id=device,
        device_id_type=pl.DeviceIdType.MESH,
    )
    copy.start()
    return copy


def sum_kernel(in_ref, out_ref, buf_y, buf_x, buf_z, acc_y, acc_x, send_sems, recv_sems):
    z, xl, y = place()
    rows = in_ref.shape[0]
    ry, rx, rz = rows // NY, rows // (NY * NXL), rows // (NY * NXL * NZ)
    to_y = [{"dp": dp_of(z, xl, (y + k) % NY)} for k in range(1, NY)]
    to_x = {"dp": dp_of(z, 1 - xl, y)}
    to_z = [{"dp": dp_of((z + k) % NZ, xl, y)} for k in range(1, NZ)]
    greet(to_y + [to_x] + to_z)

    sem = iter(range(22))

    def start(src, dst, device):
        s = next(sem)
        return send(src, dst, send_sems.at[s], recv_sems.at[s], device)

    copies = [
        start(in_ref.at[pl.ds(((y + k) % NY) * ry, ry)], buf_y.at[k - 1], to_y[k - 1])
        for k in range(1, NY)
    ]
    acc_y[...] = in_ref[pl.ds(y * ry, ry), :]
    for copy in copies:
        copy.wait()
    acc_y[...] += buf_y[0] + buf_y[1] + buf_y[2]

    copy = start(acc_y.at[pl.ds((1 - xl) * rx, rx)], buf_x, to_x)
    copy.wait()
    acc_x[...] = acc_y[pl.ds(xl * rx, rx), :] + buf_x[...]

    copies = [
        start(acc_x.at[pl.ds(((z + k) % NZ) * rz, rz)], buf_z.at[k - 1], to_z[k - 1])
        for k in range(1, NZ)
    ]
    total = acc_x[pl.ds(z * rz, rz), :]
    for k in range(NZ - 1):
        copies[k].wait()
        total = total + buf_z[k]
    base = y * ry + xl * rx
    mine = out_ref.at[pl.ds(base + z * rz, rz)]
    out_ref[pl.ds(base + z * rz, rz), :] = total
    copies = [start(mine, mine, to_z[k]) for k in range(NZ - 1)]
    for copy in copies:
        copy.wait()
    mine = out_ref.at[pl.ds(base, rx)]
    start(mine, mine, to_x).wait()
    mine = out_ref.at[pl.ds(y * ry, ry)]
    copies = [start(mine, mine, to_y[k]) for k in range(NY - 1)]
    for copy in copies:
        copy.wait()


def sum_over_dp(x):
    rows, cols = x.shape
    f32 = jnp.float32
    return pl.pallas_call(
        sum_kernel,
        out_shape=jax.ShapeDtypeStruct(x.shape, f32),
        in_specs=[pl.BlockSpec(memory_space=pltpu.VMEM)],
        out_specs=pl.BlockSpec(memory_space=pltpu.VMEM),
        scratch_shapes=[
            pltpu.VMEM((NY - 1, rows // NY, cols), f32),
            pltpu.VMEM((rows // (NY * NXL), cols), f32),
            pltpu.VMEM((NZ - 1, rows // (NY * NXL * NZ), cols), f32),
            pltpu.VMEM((rows // NY, cols), f32),
            pltpu.VMEM((rows // (NY * NXL), cols), f32),
            pltpu.SemaphoreType.DMA((22,)),
            pltpu.SemaphoreType.DMA((22,)),
        ],
        compiler_params=pltpu.CompilerParams(
            collective_id=1, has_side_effects=True, vmem_limit_bytes=40 << 20
        ),
    )(x)


ROWS = 462
HROWS = 480
HALF = HROWS // 2
BLOCKS = 4
BCOLS = 1024 // BLOCKS
N_SEMS = 300


def run_tasks(tasks):
    tasks = list(tasks)
    while tasks:
        for task in list(tasks):
            if next(task, "end") == "end":
                tasks.remove(task)


def grad_kernel(
    hid, cot, mom, basis, out, whole, H, za, C, part, came, send_sems, recv_sems, local_sem
):
    z, xl, y = place()
    mp = lax.axis_index("mp")
    xh, core = mp // 2, mp % 2
    z_dev = [{"dp": dp_of((z + k) % NZ, xl, y)} for k in range(NZ)]
    y_dev = [{"dp": dp_of(z, xl, (y + k) % NY)} for k in range(NY)]
    xl_dev = {"dp": dp_of(z, 1 - xl, y)}
    xh_dev = {"mp": (mp + 2) % 4}
    core_dev = {"mp": mp + 1 - 2 * core}
    greet(z_dev[1:] + y_dev[1:] + [xl_dev, xh_dev, core_dev])

    count = iter(range(N_SEMS))
    started = []

    def start(src, dst, device):
        s = next(count)
        copy = send(src, dst, send_sems.at[s], recv_sems.at[s], device)
        started.append(copy)
        return copy

    my_rows = pl.ds(pl.multiple_of(xh * HALF, 16), HALF)
    other_rows = pl.ds(pl.multiple_of((1 - xh) * HALF, 16), HALF)

    def lanes(zs, ys):
        return pl.ds(pl.multiple_of((zs * NY + ys) * 128, 128), 128)

    def group(zs):
        return pl.ds(pl.multiple_of(zs * 512, 512), 512)

    def hid_chunk(zd, yd):
        return hid.at[(zd * NXL + core) * NY + yd, my_rows, :]

    def hidden_task():
        mine = H.at[core, my_rows, lanes(z, y)]
        by_y = {0: [start(hid_chunk(z, (y + j) % NY), mine, y_dev[j]) for j in (1, 3, 2)]}
        by_z = {}
        order = (1, 7, 2, 6, 3, 5, 4)
        for k in order:
            zd = (z + k) % NZ
            by_z[k] = [start(hid_chunk(zd, y), mine, z_dev[k])] + [
                start(hid_chunk(zd, (y + j) % NY), za.at[z, j - 1], z_dev[k]) for j in (1, 3, 2)
            ]
        local = pltpu.make_async_copy(hid_chunk(z, y), mine, local_sem)
        local.start()
        local.wait()
        yield
        x_copies, c_copies = {}, []

        def finish(k):
            for copy in by_y[k]:
                copy.wait_recv()
            ref = H.at[core, my_rows, group((z - k + NZ) % NZ)]
            x_copies[k] = start(ref, ref, xh_dev)
            c_copies.append(start(ref, ref, core_dev))

        def cross(k):
            x_copies[k].wait_recv()
            ref = H.at[core, other_rows, group((z - k + NZ) % NZ)]
            c_copies.append(start(ref, ref, core_dev))

        seq = (0,) + order
        for i, k in enumerate(order):
            for copy in by_z[k]:
                copy.wait_recv()
            zs = (z - k + NZ) % NZ
            there = H.at[core, my_rows, lanes(zs, y)]
            by_y[k] = [start(za.at[zs, j - 1], there, y_dev[j]) for j in (1, 3, 2)]
            yield
            finish(seq[i])
            if i:
                cross(seq[i - 1])
            yield
        finish(seq[-1])
        cross(seq[-2])
        yield
        cross(seq[-1])
        for copy in c_copies:
            copy.wait_recv()

    def shard(b, zs, ys, half=None):
        first = (zs * NY + ys) * 128
        size = 128
        if half is not None:
            first, size = first + half * 64, 64
        return C.at[b, pl.ds(pl.multiple_of(first, 64), size), :]

    def gather_task(b):
        own = cot.at[:, pl.ds(b * BCOLS, BCOLS)]
        mine = shard(b, z, y)
        right, left = start(own, mine, z_dev[1]), start(own, mine, z_dev[NZ - 1])
        pushed = [(z, start(own, mine, y_dev[1]), start(own, mine, y_dev[3]))]
        C[b, pl.ds(pl.multiple_of((z * NY + y) * 128, 128), 128), :] = cot[:, b * BCOLS : (b + 1) * BCOLS]
        last = []

        def forward():
            for zi, up, down in pushed:
                up.wait_recv()
                ref = shard(b, zi, (y + 3) % NY, 0)
                last.append(start(ref, ref, y_dev[1]))
                down.wait_recv()
                ref = shard(b, zi, (y + 1) % NY, 1)
                last.append(start(ref, ref, y_dev[3]))

        for t in range(1, 5):
            yield
            right.wait_recv()
            left.wait_recv()
            low, high = (z - t + NZ) % NZ, (z + t) % NZ
            if t < 4:
                half = (0, 1) if t == 3 else (None, None)
                ref = shard(b, low, y, half[0])
                right = start(ref, ref, z_dev[1])
                ref = shard(b, high, y, half[1])
                left = start(ref, ref, z_dev[NZ - 1])
            now = []
            for zi in (low, high) if t < 4 else (low,):
                ref = shard(b, zi, y)
                now.append((zi, start(ref, ref, y_dev[1]), start(ref, ref, y_dev[3])))
            yield
            forward()
            pushed = now
        yield
        forward()
        yield
        for copy in last:
            copy.wait_recv()

    def basis_task():
        def rows_of(zs, xs, ys, n):
            return whole.at[pl.ds(pl.multiple_of(dp_of(zs, xs, ys) * 8, 8), n * 8), :]

        mine = rows_of(z, xl, y, 1)
        copies = [start(basis, mine, y_dev[j]) for j in (1, 3, 2)]
        whole[pl.ds(pl.multiple_of(dp_of(z, xl, y) * 8, 8), 8), :] = basis[...]
        yield
        for copy in copies:
            copy.wait_recv()
        mine = rows_of(z, xl, 0, NY)
        copies = {k: start(mine, mine, z_dev[k]) for k in (1, 7, 2, 6, 3, 5, 4)}
        across = [start(mine, mine, xl_dev)]
        for k, copy in copies.items():
            yield
            copy.wait_recv()
            ref = rows_of((z - k + NZ) % NZ, xl, 0, NY)
            across.append(start(ref, ref, xl_dev))
        yield
        yield
        for copy in across:
            copy.wait_recv()

    def product(b, rows):
        def step(kk, acc):
            k = pl.ds(pl.multiple_of(kk * 512, 512), 512)
            return acc + jnp.dot(H[rows, :, k], C[b, k, :], preferred_element_type=jnp.float32)

        return lax.fori_loop(0, 8, step, jnp.zeros((HROWS, BCOLS), jnp.float32))

    cross = []

    def multiply(b):
        part[b] = product(b, 1 - xl)
        cross.append(start(part.at[b], came.at[b], xl_dev))
        cols = slice(b * BCOLS, (b + 1) * BCOLS)
        out[:, cols] = mom[:, cols] + product(b, xl)[:ROWS]

    run_tasks([gather_task(b) for b in range(BLOCKS)] + [hidden_task(), basis_task()])
    for b in range(BLOCKS):
        multiply(b)
        if b:
            cross[b - 1].wait_recv()
            cols = slice((b - 1) * BCOLS, b * BCOLS)
            out[:, cols] += came[b - 1, :ROWS]
    cross[-1].wait_recv()
    cols = slice((BLOCKS - 1) * BCOLS, BLOCKS * BCOLS)
    out[:, cols] += came[BLOCKS - 1, :ROWS]
    for copy in started:
        copy.wait_send()


def merged_and_basis(hidden_t, cotangent, momentum, basis):
    bf16, f32 = jnp.bfloat16, jnp.float32
    hid = jnp.pad(hidden_t.reshape(64, ROWS, 128), ((0, 0), (0, HROWS - ROWS), (0, 0)))
    vmem = pl.BlockSpec(memory_space=pltpu.VMEM)
    return pl.pallas_call(
        grad_kernel,
        out_shape=(
            jax.ShapeDtypeStruct((ROWS, 1024), f32),
            jax.ShapeDtypeStruct((RANK, 1024), f32),
        ),
        in_specs=[pl.BlockSpec(memory_space=pl.ANY), vmem, vmem, vmem],
        out_specs=(vmem, vmem),
        scratch_shapes=[
            pltpu.VMEM((2, HROWS, 4096), bf16),
            pltpu.VMEM((NZ, NY - 1, HALF, 128), bf16),
            pltpu.VMEM((BLOCKS, 4096, BCOLS), bf16),
            pltpu.VMEM((BLOCKS, HROWS, BCOLS), f32),
            pltpu.VMEM((BLOCKS, HROWS, BCOLS), f32),
            pltpu.SemaphoreType.DMA((N_SEMS,)),
            pltpu.SemaphoreType.DMA((N_SEMS,)),
            pltpu.SemaphoreType.DMA,
        ],
        compiler_params=pltpu.CompilerParams(
            collective_id=2, has_side_effects=True, vmem_limit_bytes=56 << 20
        ),
    )(hid, cotangent, momentum, basis.T)


PB = 16

def tdot(a, b):
    return lax.dot_general(a, b, (((0,), (0,)), ((), ())), precision=lax.Precision.HIGHEST, preferred_element_type=jnp.float32)

def eliminate(R0, R1, first):
    n = R0.shape[0]
    row_id = lax.broadcasted_iota(jnp.int32, (n, 128), 0)
    cols = [jnp.broadcast_to(R0[:, first + m : first + m + 1], (n, 128)) for m in range(n)]
    pivots = jnp.ones((n, 128), jnp.float32)
    for j in range(n):
        d = jnp.broadcast_to(cols[j][j : j + 1, :], (n, 128))
        pivots = jnp.where(row_id == j, d, pivots)
        if j + 1 < n:
            f = jnp.where(row_id > j, cols[j], 0.0) * (1.0 / d)
            for m in range(j + 1, n):
                cols[m] = cols[m] - f * cols[m][j : j + 1, :]
            R0 = R0 - f * R0[j : j + 1, :]
            R1 = R1 - f * R1[j : j + 1, :]
    scale = 1.0 / jnp.sqrt(pivots)
    return R0 * scale, R1 * scale

def factor_panel(S, work, p):
    rows = pl.ds(p * 128, 128)
    work[:, :128] = S[rows, p * 128 : p * 128 + 128]
    r = lax.broadcasted_iota(jnp.int32, (128, 128), 0)
    c = lax.broadcasted_iota(jnp.int32, (128, 128), 1)
    work[:, 128:] = jnp.where(r == c, 1.0, 0.0).astype(jnp.float32)
    for b in range(128 // PB):
        lo = b * PB
        u0, u1 = eliminate(work[lo : lo + PB, :128], work[lo : lo + PB, 128:], lo)
        work[lo : lo + PB, 128:] = u1
        if b + 1 < 128 // PB:
            u = jnp.concatenate([u0, u1], axis=1)
            upd = tdot(u0, u)
            work[lo + PB :, :] = work[lo + PB :, :] - upd[lo + PB :, :]

def panel_step(S, work, p):
    factor_panel(S, work, p)
    rows = slice(p * 128, p * 128 + 128)
    end = 512 + (p + 1) * 128
    start = p * 128
    u = jnp.dot(work[:, 128:], S[rows, start:end], precision=lax.Precision.HIGHEST, preferred_element_type=jnp.float32)
    S[rows, start:end] = u
    if p < 3:
        tr = tdot(u[:, 128 : 512 - start], u[:, 128:])
        S[(p + 1) * 128 : 512, start + 128 : end] = S[(p + 1) * 128 : 512, start + 128 : end] - tr

def factor_kernel(a, x, S, work):
    S[:, :512] = a[...]
    r = lax.broadcasted_iota(jnp.int32, (512, 512), 0)
    c = lax.broadcasted_iota(jnp.int32, (512, 512), 1)
    S[:, 512:] = jnp.where(r == c, 1.0, 0.0).astype(jnp.float32)
    for p in range(4):
        panel_step(S, work, p)
    x[...] = S[:, 512:]

def inv_factor(a):
    return pl.pallas_call(factor_kernel, out_shape=jax.ShapeDtypeStruct((512, 512), jnp.float32),
        in_specs=[pl.BlockSpec(memory_space=pltpu.VMEM)], out_specs=pl.BlockSpec(memory_space=pltpu.VMEM),
        scratch_shapes=[pltpu.VMEM((512, 1024), jnp.float32), pltpu.VMEM((128, 256), jnp.float32)],
        compiler_params=pltpu.CompilerParams(vmem_limit_bytes=40 << 20))(a)


def per_device(hidden_t, cotangent, momentum, basis):
    highest = lax.Precision.HIGHEST
    merged, basis_rows = merged_and_basis(hidden_t, cotangent, momentum, basis)
    whole_basis = basis_rows.T
    left_prod = lax.psum(jnp.dot(merged, whole_basis, precision=highest), "mp")
    gram_part = jnp.dot(left_prod.T, left_prod, precision=highest)
    right_part = jnp.dot(merged.T, left_prod, precision=highest)
    sums = sum_over_dp(jnp.concatenate([right_part, gram_part], axis=0))
    gram_sum = sums[1024:]
    inverse = inv_factor(gram_sum)
    orthonormal = jnp.dot(left_prod, inverse.T, precision=highest)
    rank_share = basis.shape[1]
    right_full = jnp.dot(sums[:1024], inverse.T, precision=highest)
    squares = lax.psum(jnp.sum(right_full * right_full, axis=0), "mp")
    unit_cols = right_full / (jnp.sqrt(squares) + epsilon)
    new_basis = lax.dynamic_slice_in_dim(
        unit_cols, lax.axis_index("dp") * rank_share, rank_share, 1
    )
    new_momentum = merged - (1.0 - momentum_rate) * jnp.dot(
        orthonormal, right_full.T, precision=highest
    )
    direction_scale = (FF * D / RANK) ** 0.5
    direction = (direction_scale * jnp.dot(orthonormal, unit_cols.T, precision=highest)).astype(
        jnp.bfloat16
    )
    return (new_momentum, new_basis, direction)


def solution(mesh):
    in_specs = (P(None, "dp"), P("dp", "mp"), P("dp", "mp"), P("mp", "dp"))
    out_specs = (P("dp", "mp"), P("mp", "dp"), P("dp", "mp"))
    return jax.shard_map(
        per_device, mesh=mesh, in_specs=in_specs, out_specs=out_specs, check_vma=False
    )
```

```python
import jax
import jax.numpy as jnp
from jax import lax
from jax.experimental import pallas as pl
from jax.experimental.pallas import tpu as pltpu
from jax.sharding import PartitionSpec as P

D = 4096
FF = 29568
RANK = 512

NY, NXL, NZ = 4, 2, 8

epsilon = 1e-06
momentum_rate = 0.95


def place():
    dp = lax.axis_index("dp")
    return dp // (NXL * NY), (dp // NY) % NXL, dp % NY


def dp_of(z, xl, y):
    return (z * NXL + xl) * NY + y


def greet(partners):
    barrier = pltpu.get_barrier_semaphore()
    for device in partners:
        pl.semaphore_signal(
            barrier, inc=1, device_id=device, device_id_type=pl.DeviceIdType.MESH
        )
    pl.semaphore_wait(barrier, len(partners))


def send(src, dst, send_sem, recv_sem, device):
    copy = pltpu.make_async_remote_copy(
        src_ref=src,
        dst_ref=dst,
        send_sem=send_sem,
        recv_sem=recv_sem,
        device_id=device,
        device_id_type=pl.DeviceIdType.MESH,
    )
    copy.start()
    return copy


ROWS = 462
HROWS = 480
HALF = HROWS // 2
BLOCKS = 4
BCOLS = 1024 // BLOCKS
N_SEMS = 300


def grad_kernel(
    hid, cot, mom, basis, out, whole, H, za, C, part, came, send_sems, recv_sems, local_sem
):
    z, xl, y = place()
    mp = lax.axis_index("mp")
    xh, core = mp // 2, mp % 2
    z_dev = [{"dp": dp_of((z + k) % NZ, xl, y)} for k in range(NZ)]
    y_dev = [{"dp": dp_of(z, xl, (y + k) % NY)} for k in range(NY)]
    xl_dev = {"dp": dp_of(z, 1 - xl, y)}
    xh_dev = {"mp": (mp + 2) % 4}
    core_dev = {"mp": mp + 1 - 2 * core}
    plane_dev = [
        {"dp": dp_of(z, (xl + i) % NXL, (y + j) % NY)} for i in range(NXL) for j in range(NY)
    ]
    greet(z_dev[1:] + plane_dev[1:] + [xh_dev, core_dev])

    count = iter(range(N_SEMS))
    started = []

    def start(src, dst, device):
        s = next(count)
        copy = send(src, dst, send_sems.at[s], recv_sems.at[s], device)
        started.append(copy)
        return copy

    my_rows = pl.ds(pl.multiple_of(xh * HALF, 16), HALF)
    other_rows = pl.ds(pl.multiple_of((1 - xh) * HALF, 16), HALF)

    def lanes(zs, ys):
        return pl.ds(pl.multiple_of((zs * NY + ys) * 128, 128), 128)

    def group(zs):
        return pl.ds(pl.multiple_of(zs * 512, 512), 512)

    def first_row(d):
        return ROWS * d // 16 * 16 - d // 63 * 16

    shift = ROWS * dp_of(z, xl, y) - first_row(dp_of(z, xl, y))

    def hid_chunk(zd, yd):
        first = first_row(dp_of(zd, core, yd)) + xh * HALF
        return hid.at[pl.ds(pl.multiple_of(first, 16), HALF), :]

    def hidden_task():
        mine = H.at[core, my_rows, lanes(z, y)]
        by_y = {0: [start(hid_chunk(z, (y + j) % NY), mine, y_dev[j]) for j in (1, 3, 2)]}
        by_z, x_copies, c_copies = {}, {}, []
        pairs = [(1, 7), (2, 6), (3, 5), (4,)]

        def send_z(pair):
            for k in pair:
                zd = (z + k) % NZ
                by_z[k] = [start(hid_chunk(zd, y), mine, z_dev[k])] + [
                    start(hid_chunk(zd, (y + j) % NY), za.at[z, j - 1], z_dev[k])
                    for j in (1, 3, 2)
                ]

        def finish(pair):
            for k in pair:
                for copy in by_y[k]:
                    copy.wait_recv()
                ref = H.at[core, my_rows, group((z - k + NZ) % NZ)]
                x_copies[k] = start(ref, ref, xh_dev)
                c_copies.append(start(ref, ref, core_dev))

        def cross(pair):
            for k in pair:
                x_copies[k].wait_recv()
                ref = H.at[core, other_rows, group((z - k + NZ) % NZ)]
                c_copies.append(start(ref, ref, core_dev))

        send_z(pairs[0])
        send_z(pairs[1])
        local = pltpu.make_async_copy(hid_chunk(z, y), mine, local_sem)
        local.start()
        local.wait()
        yield
        seq = [(0,)] + pairs
        for i, pair in enumerate(pairs):
            for k in pair:
                for copy in by_z[k]:
                    copy.wait_recv()
                zs = (z - k + NZ) % NZ
                there = H.at[core, my_rows, lanes(zs, y)]
                by_y[k] = [start(za.at[zs, j - 1], there, y_dev[j]) for j in (1, 3, 2)]
            if i + 2 < len(pairs):
                send_z(pairs[i + 2])
            yield
            finish(seq[i])
            if i:
                cross(seq[i - 1])
            yield
        finish(seq[-1])
        cross(seq[-2])
        yield
        cross(seq[-1])
        yield
        for copy in c_copies:
            copy.wait_recv()

    def shard(b, zs, ys, half=None):
        first = (zs * NY + ys) * 128
        size = 128
        if half is not None:
            first, size = first + half * 64, 64
        return C.at[b, pl.ds(pl.multiple_of(first, 64), size), :]

    def gather_task(b):
        src = cot.at[:, pl.ds(b * BCOLS, BCOLS)]
        mine = shard(b, z, y)
        right, left = start(src, mine, z_dev[1]), start(src, mine, z_dev[NZ - 1])
        pushed = [(z, start(src, mine, y_dev[1]), start(src, mine, y_dev[3]))]
        C[b, pl.ds(pl.multiple_of((z * NY + y) * 128, 128), 128), :] = cot[:, b * BCOLS : (b + 1) * BCOLS]
        last = []

        def forward():
            for zi, up, down in pushed:
                up.wait_recv()
                ref = shard(b, zi, (y + 3) % NY, 0)
                last.append(start(ref, ref, y_dev[1]))
                down.wait_recv()
                ref = shard(b, zi, (y + 1) % NY, 1)
                last.append(start(ref, ref, y_dev[3]))

        for t in range(1, 5):
            yield
            right.wait_recv()
            left.wait_recv()
            low, high = (z - t + NZ) % NZ, (z + t) % NZ
            if t < 4:
                half = (0, 1) if t == 3 else (None, None)
                ref = shard(b, low, y, half[0])
                right = start(ref, ref, z_dev[1])
                ref = shard(b, high, y, half[1])
                left = start(ref, ref, z_dev[NZ - 1])
            now = []
            for zi in (low, high) if t < 4 else (low,):
                ref = shard(b, zi, y)
                now.append((zi, start(ref, ref, y_dev[1]), start(ref, ref, y_dev[3])))
            yield
            forward()
            pushed = now
        yield
        forward()
        yield
        for copy in last:
            copy.wait_recv()

    def basis_task():
        first = pl.multiple_of(dp_of(z, xl, y) * 8, 8)
        mine = whole.at[pl.ds(first, 8), :]
        copies = [start(basis, mine, plane_dev[k]) for k in range(1, 8)]
        whole[pl.ds(first, 8), :] = basis[...]
        yield
        for copy in copies:
            copy.wait_recv()

        def level(zs, half=None):
            at, size = zs * 64, 64
            if half is not None:
                at, size = at + half * 32, 32
            return whole.at[pl.ds(pl.multiple_of(at, 32), size), :]

        right, left = start(level(z), level(z), z_dev[1]), start(level(z), level(z), z_dev[NZ - 1])
        for t in range(1, 5):
            yield
            right.wait_recv()
            left.wait_recv()
            if t < 4:
                half = (0, 1) if t == 3 else (None, None)
                ref = level((z - t + NZ) % NZ, half[0])
                right = start(ref, ref, z_dev[1])
                ref = level((z + t) % NZ, half[1])
                left = start(ref, ref, z_dev[NZ - 1])

    def product(b, rows):
        def step(kk, acc):
            k = pl.ds(pl.multiple_of(kk * 512, 512), 512)
            return acc + jnp.dot(H[rows, :, k], C[b, k, :], preferred_element_type=jnp.float32)

        return lax.fori_loop(0, 8, step, jnp.zeros((HROWS, BCOLS), jnp.float32))

    cross = []

    def aligned(value):
        return pltpu.roll(value, (HROWS - shift) % HROWS, 0)[:ROWS]

    def columns(b):
        return slice(b * BCOLS, (b + 1) * BCOLS)

    def multiply(b):
        part[b] = product(b, 1 - xl)
        cross.append(start(part.at[b], came.at[b], xl_dev))
        turn()
        out[:ROWS, columns(b)] = mom[:, columns(b)] + aligned(product(b, xl))
        out[ROWS:, columns(b)] = jnp.zeros((PAD_ROWS - ROWS, BCOLS), jnp.float32)
        turn()

    def add(b):
        cross[b].wait_recv()
        out[:ROWS, columns(b)] += aligned(came[b])

    gathers = [gather_task(b) for b in range(BLOCKS)]
    hidden = hidden_task()
    running = [gathers[0], hidden, gathers[1]]
    waiting = [gathers[2], gathers[3]]
    for task in running:
        next(task)
    basis_gather = basis_task()

    def turn():
        for task in list(running):
            if next(task, "end") == "end":
                running.remove(task)
                if waiting and task is not hidden:
                    running.append(waiting.pop(0))

    turn()
    next(basis_gather)
    running.append(basis_gather)
    while hidden in running:
        turn()
    for b in range(BLOCKS):
        while gathers[b] in running or gathers[b] in waiting:
            turn()
        multiply(b)
        if b:
            add(b - 1)
    while running:
        turn()
    add(BLOCKS - 1)
    for copy in started:
        copy.wait_send()


def merged_and_basis(hidden_t, cotangent, momentum, basis):
    bf16, f32 = jnp.bfloat16, jnp.float32
    vmem = pl.BlockSpec(memory_space=pltpu.VMEM)
    return pl.pallas_call(
        grad_kernel,
        out_shape=(
            jax.ShapeDtypeStruct((PAD_ROWS, 1024), f32),
            jax.ShapeDtypeStruct((RANK, 1024), f32),
        ),
        in_specs=[pl.BlockSpec(memory_space=pl.ANY), vmem, vmem, vmem],
        out_specs=(vmem, vmem),
        scratch_shapes=[
            pltpu.VMEM((2, HROWS, 4096), bf16),
            pltpu.VMEM((NZ, NY - 1, HALF, 128), bf16),
            pltpu.VMEM((BLOCKS, 4096, BCOLS), bf16),
            pltpu.VMEM((BLOCKS, HROWS, BCOLS), f32),
            pltpu.VMEM((BLOCKS, HROWS, BCOLS), f32),
            pltpu.SemaphoreType.DMA((N_SEMS,)),
            pltpu.SemaphoreType.DMA((N_SEMS,)),
            pltpu.SemaphoreType.DMA,
        ],
        compiler_params=pltpu.CompilerParams(
            collective_id=2, has_side_effects=True, vmem_limit_bytes=56 << 20
        ),
    )(hidden_t, cotangent, momentum, basis.T)


PB = 16

def tdot(a, b):
    return lax.dot_general(a, b, (((0,), (0,)), ((), ())), precision=lax.Precision.HIGHEST, preferred_element_type=jnp.float32)

def eliminate(R0, R1, first):
    n = R0.shape[0]
    row_id = lax.broadcasted_iota(jnp.int32, (n, 128), 0)
    cols = [jnp.broadcast_to(R0[:, first + m : first + m + 1], (n, 128)) for m in range(n)]
    pivots = jnp.ones((n, 128), jnp.float32)
    for j in range(n):
        d = jnp.broadcast_to(cols[j][j : j + 1, :], (n, 128))
        pivots = jnp.where(row_id == j, d, pivots)
        if j + 1 < n:
            f = jnp.where(row_id > j, cols[j], 0.0) * (1.0 / d)
            for m in range(j + 1, n):
                cols[m] = cols[m] - f * cols[m][j : j + 1, :]
            R0 = R0 - f * R0[j : j + 1, :]
            R1 = R1 - f * R1[j : j + 1, :]
    scale = 1.0 / jnp.sqrt(pivots)
    return R0 * scale, R1 * scale

def factor_panel(S, work, p):
    rows = pl.ds(p * 128, 128)
    work[:, :128] = S[rows, p * 128 : p * 128 + 128]
    r = lax.broadcasted_iota(jnp.int32, (128, 128), 0)
    c = lax.broadcasted_iota(jnp.int32, (128, 128), 1)
    work[:, 128:] = jnp.where(r == c, 1.0, 0.0).astype(jnp.float32)
    for b in range(128 // PB):
        lo = b * PB
        u0, u1 = eliminate(work[lo : lo + PB, :128], work[lo : lo + PB, 128:], lo)
        work[lo : lo + PB, 128:] = u1
        if b + 1 < 128 // PB:
            u = jnp.concatenate([u0, u1], axis=1)
            upd = tdot(u0, u)
            work[lo + PB :, :] = work[lo + PB :, :] - upd[lo + PB :, :]

def panel_step(S, work, p):
    factor_panel(S, work, p)
    rows = slice(p * 128, p * 128 + 128)
    end = 512 + (p + 1) * 128
    start = p * 128
    u = jnp.dot(work[:, 128:], S[rows, start:end], precision=lax.Precision.HIGHEST, preferred_element_type=jnp.float32)
    S[rows, start:end] = u
    if p < 3:
        tr = tdot(u[:, 128 : 512 - start], u[:, 128:])
        S[(p + 1) * 128 : 512, start + 128 : end] = S[(p + 1) * 128 : 512, start + 128 : end] - tr

PAD_ROWS = 464
HALF_ROWS = PAD_ROWS // 2
HIGHEST = lax.Precision.HIGHEST


def dot_nt(a, b):
    return lax.dot_general(
        a, b, (((1,), (1,)), ((), ())), precision=HIGHEST, preferred_element_type=jnp.float32
    )


def update_kernel(
    merged, basis, ortho, right, unit,
    lpart, lcame, lown, lxcame, left, gram, gcame, gplane, gz, gsum, gfull, S, work,
    w, wsum, ay, ax, az, ay_acc, ax_acc, cx, cy, cz, cx_acc, cy_acc, sq, sqcame,
    send_sems, recv_sems,
):
    z, xl, y = place()
    mp = lax.axis_index("mp")
    core = mp % 2
    z_dev = [{"dp": dp_of((z + k) % NZ, xl, y)} for k in range(NZ)]
    y_dev = [{"dp": dp_of(z, xl, (y + k) % NY)} for k in range(NY)]
    x_dev = [None, {"dp": dp_of(z, 1 - xl, y)}]
    plane = [((xl + i) % NXL, (y + j) % NY) for i in range(NXL) for j in range(NY)]
    plane_dev = [{"dp": dp_of(z, a, b)} for a, b in plane]
    xh_dev = {"mp": (mp + 2) % 4}
    core_dev = {"mp": mp + 1 - 2 * core}
    far_dev = {"mp": (mp + 2) % 4 + 1 - 2 * core}
    greet(z_dev[1:] + plane_dev[1:] + [xh_dev, core_dev, far_dev])

    count = iter(range(UPDATE_SEMS))
    started = []

    def start(src, dst, device):
        s = next(count)
        copy = send(src, dst, send_sems.at[s], recv_sems.at[s], device)
        started.append(copy)
        return copy

    def rows(first, size):
        return pl.ds(pl.multiple_of(first, 8), size)

    def left_part(half):
        there = rows(half * HALF_ROWS, HALF_ROWS)

        def step(t, _):
            cols = pl.ds(pl.multiple_of(t * 256, 256), 256)
            lpart[there, cols] = dot_nt(merged[there, :], basis[cols, :])
            return 0

        lax.fori_loop(0, 2, step, 0)

    left_part(1 - core)
    swap = start(lpart.at[rows((1 - core) * HALF_ROWS, HALF_ROWS)], lcame, core_dev)
    left_part(core)
    swap.wait_recv()
    mine = rows(core * HALF_ROWS, HALF_ROWS)
    lown[...] = lpart[mine, :] + lcame[...]
    swap = start(lown, lxcame, xh_dev)
    swap.wait_recv()
    left[mine, :] = lown[...] + lxcame[...]
    left_swap = start(left.at[mine], left.at[mine], core_dev)

    def gram_step(t, _):
        cols = pl.ds(pl.multiple_of(t * 128, 128), 128)
        gram[cols, :] = tdot(left[mine, cols], left[mine, :])
        return 0

    lax.fori_loop(0, 4, gram_step, 0)
    swap = start(gram.at[rows((1 - core) * 256, 256)], gcame, core_dev)
    swap.wait_recv()
    gcame[...] = gcame[...] + gram[rows(core * 256, 256), :]
    copies = [
        start(gcame.at[rows((a * NY + b) * 32, 32)], gplane.at[k - 1], plane_dev[k])
        for k, (a, b) in enumerate(plane)
        if k
    ]
    left_swap.wait_recv()

    def w_step(t, _):
        cols = pl.ds(pl.multiple_of(t * 128, 128), 128)
        part = tdot(merged[:, cols], left[...])
        w[0, cols, :] = part[:, :256]
        w[1, cols, :] = part[:, 256:]
        return 0

    lax.fori_loop(0, 8, w_step, 0)

    def sum_task(half, axes):
        source, first, size = w.at[half], 0, 1024
        for n, me, devices, came, acc in axes:
            size = size // n
            pieces = [
                start(source.at[rows(((me + k) % n) * size, size)], came.at[k - 1], devices[k])
                for k in range(1, n)
            ]
            yield
            total = source[rows(me * size, size), :]
            for k in range(n - 1):
                pieces[k].wait_recv()
                total = total + came[k]
            first = first + me * size
            if acc is not None:
                acc[...] = total
                source = acc
        wsum[half, rows(first, size), :] = total
        for n, me, devices, came, acc in reversed(axes):
            ref = wsum.at[half, rows(first, size)]
            pieces = [start(ref, ref, devices[k]) for k in range(1, n)]
            yield
            for copy in pieces:
                copy.wait_recv()
            first = first - me * size
            size = size * n

    y_axis, x_axis, z_axis = (NY, y, y_dev), (NXL, xl, x_dev), (NZ, z, z_dev)
    sums = [
        sum_task(0, [(*y_axis, ay, ay_acc), (*x_axis, ax, ax_acc), (*z_axis, az, None)]),
        sum_task(1, [(*x_axis, cx, cx_acc), (*y_axis, cy, cy_acc), (*z_axis, cz, None)]),
    ]

    def go_on():
        for task in list(sums):
            if next(task, "end") == "end":
                sums.remove(task)

    total = gcame[rows((xl * NY + y) * 32, 32), :]
    for k in range(7):
        copies[k].wait_recv()
        total = total + gplane[k]
    gsum[...] = total

    def z_block(ref, i):
        return ref.at[rows((i // 2) * 8, 8), pl.ds(pl.multiple_of((i % 2) * 256, 256), 256)]

    copies = [
        start(z_block(gsum, (z + k) % NZ), gz.at[k - 1], z_dev[k]) for k in range(1, NZ)
    ]
    go_on()
    my_block = z_block(gsum, z)
    total = my_block[...]
    for k in range(7):
        copies[k].wait_recv()
        total = total + gz[k]
    base = core * 256 + (xl * NY + y) * 32
    here = z_block(gfull.at[rows(base, 32)], z)
    here[...] = total
    copies = [start(here, here, z_dev[k]) for k in range(1, NZ)]
    for copy in copies:
        copy.wait_recv()
    here = gfull.at[rows(base, 32)]
    copies = [start(here, here, plane_dev[k]) for k in range(1, 8)]
    for copy in copies:
        copy.wait_recv()
    here = gfull.at[rows(core * 256, 256)]
    swap = start(here, here, core_dev)
    swap.wait_recv()

    S[:, :512] = gfull[...]
    r = lax.broadcasted_iota(jnp.int32, (512, 512), 0)
    c = lax.broadcasted_iota(jnp.int32, (512, 512), 1)
    S[:, 512:] = jnp.where(r == c, 1.0, 0.0).astype(jnp.float32)
    for p in range(4):
        panel_step(S, work, p)
        go_on()
    while sums:
        go_on()

    def right_step(t, total):
        here = pl.ds(pl.multiple_of(t * 128, 128), 128)
        both = jnp.concatenate([wsum[0, here, :], wsum[1, here, :]], axis=1)
        value = dot_nt(both, S[:, 512:])
        right[here, :] = value
        return total + jnp.sum((value * value).reshape(16, 8, 512), axis=0)

    total = lax.fori_loop(0, 8, right_step, jnp.zeros((8, 512), jnp.float32))
    sq[...] = total
    copies = [
        start(sq, sqcame.at[i], device) for i, device in enumerate([core_dev, xh_dev, far_dev])
    ]

    def ortho_step(t, _):
        here = pl.ds(pl.multiple_of(t * HALF_ROWS, 8), HALF_ROWS)
        ortho[here, :] = dot_nt(left[here, :], S[:, 512:])
        return 0

    lax.fori_loop(0, 2, ortho_step, 0)
    for copy in copies:
        copy.wait_recv()
    squares = jnp.sum(sq[...] + sqcame[0] + sqcame[1] + sqcame[2], axis=0, keepdims=True)
    unit[...] = right[...] * (1.0 / (jnp.sqrt(squares) + epsilon))
    for copy in started:
        copy.wait_send()


UPDATE_SEMS = 100


def low_rank_update(merged, basis_rows):
    f32 = jnp.float32
    vmem = pl.BlockSpec(memory_space=pltpu.VMEM)

    def buffer(*shape):
        return pltpu.VMEM(shape, f32)

    return pl.pallas_call(
        update_kernel,
        out_shape=(
            jax.ShapeDtypeStruct((PAD_ROWS, RANK), f32),
            jax.ShapeDtypeStruct((1024, RANK), f32),
            jax.ShapeDtypeStruct((1024, RANK), f32),
        ),
        in_specs=[vmem, vmem],
        out_specs=(vmem, vmem, vmem),
        scratch_shapes=[
            buffer(PAD_ROWS, RANK),
            buffer(HALF_ROWS, RANK),
            buffer(HALF_ROWS, RANK),
            buffer(HALF_ROWS, RANK),
            buffer(PAD_ROWS, RANK),
            buffer(RANK, RANK),
            buffer(256, RANK),
            buffer(7, 32, RANK),
            buffer(7, 8, 256),
            buffer(32, RANK),
            buffer(RANK, RANK),
            buffer(RANK, 2 * RANK),
            buffer(128, 256),
            buffer(2, 1024, 256),
            buffer(2, 1024, 256),
            buffer(3, 256, 256),
            buffer(1, 128, 256),
            buffer(7, 16, 256),
            buffer(256, 256),
            buffer(128, 256),
            buffer(1, 512, 256),
            buffer(3, 128, 256),
            buffer(7, 16, 256),
            buffer(512, 256),
            buffer(128, 256),
            buffer(8, RANK),
            buffer(3, 8, RANK),
            pltpu.SemaphoreType.DMA((UPDATE_SEMS,)),
            pltpu.SemaphoreType.DMA((UPDATE_SEMS,)),
        ],
        compiler_params=pltpu.CompilerParams(
            collective_id=1, has_side_effects=True, vmem_limit_bytes=50 << 20
        ),
    )(merged, basis_rows)


def per_device(hidden_t, cotangent, momentum, basis):
    high = lax.Precision.HIGH
    merged, basis_rows = merged_and_basis(hidden_t, cotangent, momentum, basis)
    orthonormal, right_full, unit_cols = low_rank_update(merged, basis_rows)
    merged, orthonormal = merged[:ROWS], orthonormal[:ROWS]
    rank_share = basis.shape[1]
    new_basis = lax.dynamic_slice_in_dim(
        unit_cols, lax.axis_index("dp") * rank_share, rank_share, 1
    )
    new_momentum = merged - (1.0 - momentum_rate) * jnp.dot(
        orthonormal, right_full.T, precision=high
    )
    direction_scale = (FF * D / RANK) ** 0.5
    direction = (direction_scale * jnp.dot(orthonormal, unit_cols.T, precision=high)).astype(
        jnp.bfloat16
    )
    return (new_momentum, new_basis, direction)


def solution(mesh):
    in_specs = (P(None, "dp"), P("dp", "mp"), P("dp", "mp"), P("mp", "dp"))
    out_specs = (P("dp", "mp"), P("mp", "dp"), P("dp", "mp"))
    return jax.shard_map(
        per_device, mesh=mesh, in_specs=in_specs, out_specs=out_specs, check_vma=False
    )
```

```python
import jax
import jax.numpy as jnp
from jax import lax
from jax.experimental import pallas as pl
from jax.experimental.pallas import tpu as pltpu
from jax.sharding import PartitionSpec as P

D = 4096
FF = 29568
RANK = 512

NY, NXL, NZ = 4, 2, 8

epsilon = 1e-06
momentum_rate = 0.95


def place():
    dp = lax.axis_index("dp")
    return dp // (NXL * NY), (dp // NY) % NXL, dp % NY


def dp_of(z, xl, y):
    return (z * NXL + xl) * NY + y


def greet(partners):
    barrier = pltpu.get_barrier_semaphore()
    for device in partners:
        pl.semaphore_signal(
            barrier, inc=1, device_id=device, device_id_type=pl.DeviceIdType.MESH
        )
    pl.semaphore_wait(barrier, len(partners))


def send(src, dst, send_sem, recv_sem, device):
    copy = pltpu.make_async_remote_copy(
        src_ref=src,
        dst_ref=dst,
        send_sem=send_sem,
        recv_sem=recv_sem,
        device_id=device,
        device_id_type=pl.DeviceIdType.MESH,
    )
    copy.start()
    return copy


ROWS = 462
HROWS = 480
HALF = HROWS // 2
BLOCKS = 4
BCOLS = 1024 // BLOCKS
N_SEMS = 300
DEPTH = 2048


def grad_kernel(
    hid, cot, mom, basis, out, whole, H, za, C, part, came, send_sems, recv_sems, local_sem
):
    z, xl, y = place()
    mp = lax.axis_index("mp")
    xh, core = mp // 2, mp % 2
    z_dev = [{"dp": dp_of((z + k) % NZ, xl, y)} for k in range(NZ)]
    y_dev = [{"dp": dp_of(z, xl, (y + k) % NY)} for k in range(NY)]
    xl_dev = {"dp": dp_of(z, 1 - xl, y)}
    xh_dev = {"mp": (mp + 2) % 4}
    core_dev = {"mp": mp + 1 - 2 * core}
    plane_dev = [
        {"dp": dp_of(z, (xl + i) % NXL, (y + j) % NY)} for i in range(NXL) for j in range(NY)
    ]
    greet(z_dev[1:] + plane_dev[1:] + [xh_dev, core_dev])

    count = iter(range(N_SEMS))
    started = []

    def start(src, dst, device):
        s = next(count)
        copy = send(src, dst, send_sems.at[s], recv_sems.at[s], device)
        started.append(copy)
        return copy

    my_rows = pl.ds(pl.multiple_of(xh * HALF, 16), HALF)
    other_rows = pl.ds(pl.multiple_of((1 - xh) * HALF, 16), HALF)

    def lanes(zs, ys):
        return pl.ds(pl.multiple_of((zs * NY + ys) * 128, 128), 128)

    def group(zs):
        return pl.ds(pl.multiple_of(zs * 512, 512), 512)

    def first_row(d):
        return ROWS * d // 16 * 16 - d // 63 * 16

    shift = ROWS * dp_of(z, xl, y) - first_row(dp_of(z, xl, y))

    def hid_chunk(zd, yd):
        first = first_row(dp_of(zd, core, yd)) + xh * HALF
        return hid.at[pl.ds(pl.multiple_of(first, 16), HALF), :]

    def hidden_task():
        mine = H.at[core, my_rows, lanes(z, y)]
        by_y = {0: [start(hid_chunk(z, (y + j) % NY), mine, y_dev[j]) for j in (1, 3, 2)]}
        by_z, x_copies, c_copies = {}, {}, []
        pairs = [(1, 7), (2, 6), (3, 5), (4,)]

        def send_z(pair):
            for k in pair:
                zd = (z + k) % NZ
                by_z[k] = [start(hid_chunk(zd, y), mine, z_dev[k])] + [
                    start(hid_chunk(zd, (y + j) % NY), za.at[z, j - 1], z_dev[k])
                    for j in (1, 3, 2)
                ]

        def finish(pair):
            for k in pair:
                for copy in by_y[k]:
                    copy.wait_recv()
                ref = H.at[core, my_rows, group((z - k + NZ) % NZ)]
                x_copies[k] = start(ref, ref, xh_dev)
                c_copies.append(start(ref, ref, core_dev))

        def cross(pair):
            for k in pair:
                x_copies[k].wait_recv()
                ref = H.at[core, other_rows, group((z - k + NZ) % NZ)]
                c_copies.append(start(ref, ref, core_dev))

        send_z(pairs[0])
        send_z(pairs[1])
        local = pltpu.make_async_copy(hid_chunk(z, y), mine, local_sem)
        local.start()
        local.wait()
        yield
        seq = [(0,)] + pairs
        for i, pair in enumerate(pairs):
            for k in pair:
                for copy in by_z[k]:
                    copy.wait_recv()
                zs = (z - k + NZ) % NZ
                there = H.at[core, my_rows, lanes(zs, y)]
                by_y[k] = [start(za.at[zs, j - 1], there, y_dev[j]) for j in (1, 3, 2)]
            if i + 2 < len(pairs):
                send_z(pairs[i + 2])
            yield
            finish(seq[i])
            if i:
                cross(seq[i - 1])
            yield
        finish(seq[-1])
        cross(seq[-2])
        yield
        cross(seq[-1])
        yield
        for copy in c_copies:
            copy.wait_recv()

    def shard(b, zs, ys, half=None):
        first = (zs * NY + ys) * 128
        size = 128
        if half is not None:
            first, size = first + half * 64, 64
        return C.at[b, pl.ds(pl.multiple_of(first, 64), size), :]

    def gather_task(b):
        src = cot.at[:, pl.ds(b * BCOLS, BCOLS)]
        mine = shard(b, z, y)
        right, left = start(src, mine, z_dev[1]), start(src, mine, z_dev[NZ - 1])
        pushed = [(z, start(src, mine, y_dev[1]), start(src, mine, y_dev[3]))]
        C[b, pl.ds(pl.multiple_of((z * NY + y) * 128, 128), 128), :] = cot[:, b * BCOLS : (b + 1) * BCOLS]
        last = []

        def forward():
            for zi, up, down in pushed:
                up.wait_recv()
                ref = shard(b, zi, (y + 3) % NY, 0)
                last.append(start(ref, ref, y_dev[1]))
                down.wait_recv()
                ref = shard(b, zi, (y + 1) % NY, 1)
                last.append(start(ref, ref, y_dev[3]))

        for t in range(1, 5):
            yield
            right.wait_recv()
            left.wait_recv()
            low, high = (z - t + NZ) % NZ, (z + t) % NZ
            if t < 4:
                half = (0, 1) if t == 3 else (None, None)
                ref = shard(b, low, y, half[0])
                right = start(ref, ref, z_dev[1])
                ref = shard(b, high, y, half[1])
                left = start(ref, ref, z_dev[NZ - 1])
            now = []
            for zi in (low, high) if t < 4 else (low,):
                ref = shard(b, zi, y)
                now.append((zi, start(ref, ref, y_dev[1]), start(ref, ref, y_dev[3])))
            yield
            forward()
            pushed = now
        yield
        forward()
        yield
        for copy in last:
            copy.wait_recv()

    def basis_task():
        first = pl.multiple_of(dp_of(z, xl, y) * 8, 8)
        mine = whole.at[pl.ds(first, 8), :]
        copies = [start(basis, mine, plane_dev[k]) for k in range(1, 8)]
        whole[pl.ds(first, 8), :] = basis[...]
        yield
        for copy in copies:
            copy.wait_recv()

        def level(zs, half=None):
            at, size = zs * 64, 64
            if half is not None:
                at, size = at + half * 32, 32
            return whole.at[pl.ds(pl.multiple_of(at, 32), size), :]

        right, left = start(level(z), level(z), z_dev[1]), start(level(z), level(z), z_dev[NZ - 1])
        for t in range(1, 5):
            yield
            right.wait_recv()
            left.wait_recv()
            if t < 4:
                half = (0, 1) if t == 3 else (None, None)
                ref = level((z - t + NZ) % NZ, half[0])
                right = start(ref, ref, z_dev[1])
                ref = level((z + t) % NZ, half[1])
                left = start(ref, ref, z_dev[NZ - 1])

    def product(b, rows):
        def step(kk, acc):
            k = pl.ds(pl.multiple_of(kk * DEPTH, DEPTH), DEPTH)
            return acc + jnp.dot(H[rows, :, k], C[b, k, :], preferred_element_type=jnp.float32)

        return lax.fori_loop(0, 4096 // DEPTH, step, jnp.zeros((HROWS, BCOLS), jnp.float32))

    cross = []

    def aligned(value):
        return pltpu.roll(value, (HROWS - shift) % HROWS, 0)[:ROWS]

    def columns(b):
        return slice(b * BCOLS, (b + 1) * BCOLS)

    def multiply(b):
        part[b] = product(b, 1 - xl)
        cross.append(start(part.at[b], came.at[b], xl_dev))
        turn()
        out[:ROWS, columns(b)] = mom[:, columns(b)] + aligned(product(b, xl))
        out[ROWS:, columns(b)] = jnp.zeros((PAD_ROWS - ROWS, BCOLS), jnp.float32)
        turn()

    def add(b):
        cross[b].wait_recv()
        out[:ROWS, columns(b)] += aligned(came[b])

    gathers = [gather_task(b) for b in range(BLOCKS)]
    hidden = hidden_task()
    running = [gathers[0], hidden, *gathers[1:]]
    for task in running:
        next(task)
    basis_gather = basis_task()

    def turn():
        for task in list(running):
            if next(task, "end") == "end":
                running.remove(task)


    turn()
    next(basis_gather)
    running.append(basis_gather)
    while hidden in running:
        turn()
    for b in range(BLOCKS):
        while gathers[b] in running:
            turn()
        multiply(b)
        if b:
            add(b - 1)
    while running:
        turn()
    add(BLOCKS - 1)
    for copy in started:
        copy.wait_send()


def merged_and_basis(hidden_t, cotangent, momentum, basis):
    bf16, f32 = jnp.bfloat16, jnp.float32
    vmem = pl.BlockSpec(memory_space=pltpu.VMEM)
    return pl.pallas_call(
        grad_kernel,
        out_shape=(
            jax.ShapeDtypeStruct((PAD_ROWS, 1024), f32),
            jax.ShapeDtypeStruct((RANK, 1024), f32),
        ),
        in_specs=[pl.BlockSpec(memory_space=pl.ANY), vmem, vmem, vmem],
        out_specs=(vmem, vmem),
        scratch_shapes=[
            pltpu.VMEM((2, HROWS, 4096), bf16),
            pltpu.VMEM((NZ, NY - 1, HALF, 128), bf16),
            pltpu.VMEM((BLOCKS, 4096, BCOLS), bf16),
            pltpu.VMEM((BLOCKS, HROWS, BCOLS), f32),
            pltpu.VMEM((BLOCKS, HROWS, BCOLS), f32),
            pltpu.SemaphoreType.DMA((N_SEMS,)),
            pltpu.SemaphoreType.DMA((N_SEMS,)),
            pltpu.SemaphoreType.DMA,
        ],
        compiler_params=pltpu.CompilerParams(
            collective_id=2, has_side_effects=True, vmem_limit_bytes=56 << 20
        ),
    )(hidden_t, cotangent, momentum, basis.T)


PB = 16

def tdot(a, b):
    return lax.dot_general(a, b, (((0,), (0,)), ((), ())), precision=lax.Precision.HIGHEST, preferred_element_type=jnp.float32)

def eliminate(R0, R1, first):
    n = R0.shape[0]
    row_id = lax.broadcasted_iota(jnp.int32, (n, 128), 0)
    cols = [jnp.broadcast_to(R0[:, first + m : first + m + 1], (n, 128)) for m in range(n)]
    pivots = jnp.ones((n, 128), jnp.float32)
    for j in range(n):
        d = jnp.broadcast_to(cols[j][j : j + 1, :], (n, 128))
        pivots = jnp.where(row_id == j, d, pivots)
        if j + 1 < n:
            f = jnp.where(row_id > j, cols[j], 0.0) * (1.0 / d)
            for m in range(j + 1, n):
                cols[m] = cols[m] - f * cols[m][j : j + 1, :]
            R0 = R0 - f * R0[j : j + 1, :]
            R1 = R1 - f * R1[j : j + 1, :]
    scale = 1.0 / jnp.sqrt(pivots)
    return R0 * scale, R1 * scale

def factor_panel(S, work, p):
    rows = pl.ds(p * 128, 128)
    work[:, :128] = S[rows, p * 128 : p * 128 + 128]
    r = lax.broadcasted_iota(jnp.int32, (128, 128), 0)
    c = lax.broadcasted_iota(jnp.int32, (128, 128), 1)
    work[:, 128:] = jnp.where(r == c, 1.0, 0.0).astype(jnp.float32)
    for b in range(128 // PB):
        lo = b * PB
        u0, u1 = eliminate(work[lo : lo + PB, :128], work[lo : lo + PB, 128:], lo)
        work[lo : lo + PB, 128:] = u1
        if b + 1 < 128 // PB:
            u = jnp.concatenate([u0, u1], axis=1)
            upd = tdot(u0, u)
            work[lo + PB :, :] = work[lo + PB :, :] - upd[lo + PB :, :]

def panel_step(S, work, p):
    factor_panel(S, work, p)
    rows = slice(p * 128, p * 128 + 128)
    end = 512 + (p + 1) * 128
    start = p * 128
    u = jnp.dot(work[:, 128:], S[rows, start:end], precision=lax.Precision.HIGHEST, preferred_element_type=jnp.float32)
    S[rows, start:end] = u
    if p < 3:
        tr = tdot(u[:, 128 : 512 - start], u[:, 128:])
        S[(p + 1) * 128 : 512, start + 128 : end] = S[(p + 1) * 128 : 512, start + 128 : end] - tr

PAD_ROWS = 464
HALF_ROWS = PAD_ROWS // 2
HIGHEST = lax.Precision.HIGHEST


def dot_nt(a, b):
    return lax.dot_general(
        a, b, (((1,), (1,)), ((), ())), precision=HIGHEST, preferred_element_type=jnp.float32
    )


def update_kernel(
    merged, basis, ortho, right, unit,
    lpart, lcame, lown, lxcame, left, gram, gcame, gplane, gz, gsum, gfull, S, work,
    w, wsum, ay, ax, az, ay_acc, ax_acc, cx, cy, cz, cx_acc, cy_acc, sq, sqcame,
    send_sems, recv_sems,
):
    z, xl, y = place()
    mp = lax.axis_index("mp")
    core = mp % 2
    z_dev = [{"dp": dp_of((z + k) % NZ, xl, y)} for k in range(NZ)]
    y_dev = [{"dp": dp_of(z, xl, (y + k) % NY)} for k in range(NY)]
    x_dev = [None, {"dp": dp_of(z, 1 - xl, y)}]
    plane = [((xl + i) % NXL, (y + j) % NY) for i in range(NXL) for j in range(NY)]
    plane_dev = [{"dp": dp_of(z, a, b)} for a, b in plane]
    xh_dev = {"mp": (mp + 2) % 4}
    core_dev = {"mp": mp + 1 - 2 * core}
    far_dev = {"mp": (mp + 2) % 4 + 1 - 2 * core}
    greet(z_dev[1:] + plane_dev[1:] + [xh_dev, core_dev, far_dev])

    count = iter(range(UPDATE_SEMS))
    started = []

    def start(src, dst, device):
        s = next(count)
        copy = send(src, dst, send_sems.at[s], recv_sems.at[s], device)
        started.append(copy)
        return copy

    def rows(first, size):
        return pl.ds(pl.multiple_of(first, 8), size)

    def left_part(half):
        there = rows(half * HALF_ROWS, HALF_ROWS)

        def step(t, _):
            cols = pl.ds(pl.multiple_of(t * 256, 256), 256)
            lpart[there, cols] = dot_nt(merged[there, :], basis[cols, :])
            return 0

        lax.fori_loop(0, 2, step, 0)

    left_part(1 - core)
    swap = start(lpart.at[rows((1 - core) * HALF_ROWS, HALF_ROWS)], lcame, core_dev)
    left_part(core)
    swap.wait_recv()
    mine = rows(core * HALF_ROWS, HALF_ROWS)
    lown[...] = lpart[mine, :] + lcame[...]
    swap = start(lown, lxcame, xh_dev)
    swap.wait_recv()
    left[mine, :] = lown[...] + lxcame[...]
    left_swap = start(left.at[mine], left.at[mine], core_dev)

    def gram_step(t, _):
        cols = pl.ds(pl.multiple_of(t * 128, 128), 128)
        gram[cols, :] = tdot(left[mine, cols], left[mine, :])
        return 0

    lax.fori_loop(0, 4, gram_step, 0)
    swap = start(gram.at[rows((1 - core) * 256, 256)], gcame, core_dev)
    swap.wait_recv()
    gcame[...] = gcame[...] + gram[rows(core * 256, 256), :]
    copies = [
        start(gcame.at[rows((a * NY + b) * 32, 32)], gplane.at[k - 1], plane_dev[k])
        for k, (a, b) in enumerate(plane)
        if k
    ]
    left_swap.wait_recv()

    def w_step(t, _):
        cols = pl.ds(pl.multiple_of(t * 128, 128), 128)
        part = tdot(merged[:, cols], left[...])
        w[0, cols, :] = part[:, :256]
        w[1, cols, :] = part[:, 256:]
        return 0

    lax.fori_loop(0, 8, w_step, 0)

    def sum_task(half, axes):
        source, first, size = w.at[half], 0, 1024
        for n, me, devices, came, acc in axes:
            size = size // n
            pieces = [
                start(source.at[rows(((me + k) % n) * size, size)], came.at[k - 1], devices[k])
                for k in range(1, n)
            ]
            yield
            total = source[rows(me * size, size), :]
            for k in range(n - 1):
                pieces[k].wait_recv()
                total = total + came[k]
            first = first + me * size
            if acc is not None:
                acc[...] = total
                source = acc
        wsum[half, rows(first, size), :] = total
        for n, me, devices, came, acc in reversed(axes):
            ref = wsum.at[half, rows(first, size)]
            pieces = [start(ref, ref, devices[k]) for k in range(1, n)]
            yield
            for copy in pieces:
                copy.wait_recv()
            first = first - me * size
            size = size * n

    y_axis, x_axis, z_axis = (NY, y, y_dev), (NXL, xl, x_dev), (NZ, z, z_dev)
    sums = [
        sum_task(0, [(*y_axis, ay, ay_acc), (*x_axis, ax, ax_acc), (*z_axis, az, None)]),
        sum_task(1, [(*x_axis, cx, cx_acc), (*y_axis, cy, cy_acc), (*z_axis, cz, None)]),
    ]

    def go_on():
        for task in list(sums):
            if next(task, "end") == "end":
                sums.remove(task)

    total = gcame[rows((xl * NY + y) * 32, 32), :]
    for k in range(7):
        copies[k].wait_recv()
        total = total + gplane[k]
    gsum[...] = total

    def z_block(ref, i):
        return ref.at[rows((i // 2) * 8, 8), pl.ds(pl.multiple_of((i % 2) * 256, 256), 256)]

    copies = [
        start(z_block(gsum, (z + k) % NZ), gz.at[k - 1], z_dev[k]) for k in range(1, NZ)
    ]
    go_on()
    my_block = z_block(gsum, z)
    total = my_block[...]
    for k in range(7):
        copies[k].wait_recv()
        total = total + gz[k]
    base = core * 256 + (xl * NY + y) * 32
    here = z_block(gfull.at[rows(base, 32)], z)
    here[...] = total
    copies = [start(here, here, z_dev[k]) for k in range(1, NZ)]
    for copy in copies:
        copy.wait_recv()
    here = gfull.at[rows(base, 32)]
    copies = [start(here, here, plane_dev[k]) for k in range(1, 8)]
    go_on()
    for copy in copies:
        copy.wait_recv()
    here = gfull.at[rows(core * 256, 256)]
    swap = start(here, here, core_dev)
    go_on()
    swap.wait_recv()

    S[:, :512] = gfull[...]
    r = lax.broadcasted_iota(jnp.int32, (512, 512), 0)
    c = lax.broadcasted_iota(jnp.int32, (512, 512), 1)
    S[:, 512:] = jnp.where(r == c, 1.0, 0.0).astype(jnp.float32)
    for p in range(4):
        panel_step(S, work, p)
        go_on()
    while sums:
        go_on()

    def right_step(t, total):
        here = pl.ds(pl.multiple_of(t * 128, 128), 128)
        both = jnp.concatenate([wsum[0, here, :], wsum[1, here, :]], axis=1)
        value = dot_nt(both, S[:, 512:])
        right[here, :] = value
        return total + jnp.sum((value * value).reshape(16, 8, 512), axis=0)

    total = lax.fori_loop(0, 8, right_step, jnp.zeros((8, 512), jnp.float32))
    sq[...] = total
    copies = [
        start(sq, sqcame.at[i], device) for i, device in enumerate([core_dev, xh_dev, far_dev])
    ]

    def ortho_step(t, _):
        here = pl.ds(pl.multiple_of(t * HALF_ROWS, 8), HALF_ROWS)
        ortho[here, :] = dot_nt(left[here, :], S[:, 512:])
        return 0

    lax.fori_loop(0, 2, ortho_step, 0)
    for copy in copies:
        copy.wait_recv()
    squares = jnp.sum(sq[...] + sqcame[0] + sqcame[1] + sqcame[2], axis=0, keepdims=True)
    unit[...] = right[...] * (1.0 / (jnp.sqrt(squares) + epsilon))
    for copy in started:
        copy.wait_send()


UPDATE_SEMS = 100


def low_rank_update(merged, basis_rows):
    f32 = jnp.float32
    vmem = pl.BlockSpec(memory_space=pltpu.VMEM)

    def buffer(*shape):
        return pltpu.VMEM(shape, f32)

    return pl.pallas_call(
        update_kernel,
        out_shape=(
            jax.ShapeDtypeStruct((PAD_ROWS, RANK), f32),
            jax.ShapeDtypeStruct((1024, RANK), f32),
            jax.ShapeDtypeStruct((1024, RANK), f32),
        ),
        in_specs=[vmem, vmem],
        out_specs=(vmem, vmem, vmem),
        scratch_shapes=[
            buffer(PAD_ROWS, RANK),
            buffer(HALF_ROWS, RANK),
            buffer(HALF_ROWS, RANK),
            buffer(HALF_ROWS, RANK),
            buffer(PAD_ROWS, RANK),
            buffer(RANK, RANK),
            buffer(256, RANK),
            buffer(7, 32, RANK),
            buffer(7, 8, 256),
            buffer(32, RANK),
            buffer(RANK, RANK),
            buffer(RANK, 2 * RANK),
            buffer(128, 256),
            buffer(2, 1024, 256),
            buffer(2, 1024, 256),
            buffer(3, 256, 256),
            buffer(1, 128, 256),
            buffer(7, 16, 256),
            buffer(256, 256),
            buffer(128, 256),
            buffer(1, 512, 256),
            buffer(3, 128, 256),
            buffer(7, 16, 256),
            buffer(512, 256),
            buffer(128, 256),
            buffer(8, RANK),
            buffer(3, 8, RANK),
            pltpu.SemaphoreType.DMA((UPDATE_SEMS,)),
            pltpu.SemaphoreType.DMA((UPDATE_SEMS,)),
        ],
        compiler_params=pltpu.CompilerParams(
            collective_id=1, has_side_effects=True, vmem_limit_bytes=50 << 20
        ),
    )(merged, basis_rows)


def per_device(hidden_t, cotangent, momentum, basis):
    high = lax.Precision.HIGH
    merged, basis_rows = merged_and_basis(hidden_t, cotangent, momentum, basis)
    orthonormal, right_full, unit_cols = low_rank_update(merged, basis_rows)
    merged, orthonormal = merged[:ROWS], orthonormal[:ROWS]
    rank_share = basis.shape[1]
    new_basis = lax.dynamic_slice_in_dim(
        unit_cols, lax.axis_index("dp") * rank_share, rank_share, 1
    )
    new_momentum = merged - (1.0 - momentum_rate) * jnp.dot(
        orthonormal, right_full.T, precision=high
    )
    direction_scale = (FF * D / RANK) ** 0.5
    direction = (direction_scale * jnp.dot(orthonormal, unit_cols.T, precision=high)).astype(
        jnp.bfloat16
    )
    return (new_momentum, new_basis, direction)


def solution(mesh):
    in_specs = (P(None, "dp"), P("dp", "mp"), P("dp", "mp"), P("mp", "dp"))
    out_specs = (P("dp", "mp"), P("mp", "dp"), P("dp", "mp"))
    return jax.shard_map(
        per_device, mesh=mesh, in_specs=in_specs, out_specs=out_specs, check_vma=False
    )
```

```python
import jax
import jax.numpy as jnp
from jax import lax
from jax.experimental import pallas as pl
from jax.experimental.pallas import tpu as pltpu
from jax.sharding import PartitionSpec as P

D = 4096
FF = 29568
RANK = 512

NY, NXL, NZ = 4, 2, 8

epsilon = 1e-06
momentum_rate = 0.95


def place():
    dp = lax.axis_index("dp")
    return dp // (NXL * NY), (dp // NY) % NXL, dp % NY


def dp_of(z, xl, y):
    return (z * NXL + xl) * NY + y


def greet(partners):
    barrier = pltpu.get_barrier_semaphore()
    for device in partners:
        pl.semaphore_signal(
            barrier, inc=1, device_id=device, device_id_type=pl.DeviceIdType.MESH
        )
    pl.semaphore_wait(barrier, len(partners))


def send(src, dst, send_sem, recv_sem, device):
    copy = pltpu.make_async_remote_copy(
        src_ref=src,
        dst_ref=dst,
        send_sem=send_sem,
        recv_sem=recv_sem,
        device_id=device,
        device_id_type=pl.DeviceIdType.MESH,
    )
    copy.start()
    return copy


ROWS = 462
HROWS = 480
HALF = HROWS // 2
BLOCKS = 4
BCOLS = 1024 // BLOCKS
N_SEMS = 260
DEPTH = 2048


def grad_kernel(
    hid, cot, mom, basis, out, whole, H, za, C, part, came, send_sems, recv_sems, local_sem
):
    z, xl, y = place()
    mp = lax.axis_index("mp")
    xh, core = mp // 2, mp % 2
    z_dev = [{"dp": dp_of((z + k) % NZ, xl, y)} for k in range(NZ)]
    y_dev = [{"dp": dp_of(z, xl, (y + k) % NY)} for k in range(NY)]
    xl_dev = {"dp": dp_of(z, 1 - xl, y)}
    xh_dev = {"mp": (mp + 2) % 4}
    core_dev = {"mp": mp + 1 - 2 * core}
    plane_dev = [
        {"dp": dp_of(z, (xl + i) % NXL, (y + j) % NY)} for i in range(NXL) for j in range(NY)
    ]
    far_dev = {"mp": (mp + 2) % 4 + 1 - 2 * core}
    greet(z_dev[1:] + plane_dev[1:] + [xh_dev, core_dev, far_dev])

    count = iter(range(N_SEMS))
    started = []

    def start(src, dst, device):
        s = next(count)
        copy = send(src, dst, send_sems.at[s], recv_sems.at[s], device)
        started.append(copy)
        return copy

    my_rows = pl.ds(pl.multiple_of(xh * HALF, 16), HALF)
    other_rows = pl.ds(pl.multiple_of((1 - xh) * HALF, 16), HALF)

    def lanes(zs, ys):
        return pl.ds(pl.multiple_of((zs * NY + ys) * 128, 128), 128)

    def group(zs):
        return pl.ds(pl.multiple_of(zs * 512, 512), 512)

    def first_row(d):
        return ROWS * d // 16 * 16 - d // 63 * 16

    shift = ROWS * dp_of(z, xl, y) - first_row(dp_of(z, xl, y))

    def hid_chunk(zd, yd):
        first = first_row(dp_of(zd, core, yd)) + xh * HALF
        return hid.at[pl.ds(pl.multiple_of(first, 16), HALF), :]

    def hidden_task():
        mine = H.at[core, my_rows, lanes(z, y)]
        by_y = {0: [start(hid_chunk(z, (y + j) % NY), mine, y_dev[j]) for j in (1, 3, 2)]}
        by_z, x_copies, c_copies = {}, {}, []
        pairs = [(1, 7), (2, 6), (3, 5), (4,)]

        def send_z(pair):
            for k in pair:
                zd = (z + k) % NZ
                by_z[k] = [start(hid_chunk(zd, y), mine, z_dev[k])] + [
                    start(hid_chunk(zd, (y + j) % NY), za.at[z, j - 1], z_dev[k])
                    for j in (1, 3, 2)
                ]

        def finish(pair):
            for k in pair:
                for copy in by_y[k]:
                    copy.wait_recv()
                ref = H.at[core, my_rows, group((z - k + NZ) % NZ)]
                x_copies[k] = start(ref, ref, xh_dev)
                c_copies.append(start(ref, ref, core_dev))

        def cross(pair):
            for k in pair:
                x_copies[k].wait_recv()
                ref = H.at[core, other_rows, group((z - k + NZ) % NZ)]
                c_copies.append(start(ref, ref, core_dev))

        send_z(pairs[0])
        send_z(pairs[1])
        local = pltpu.make_async_copy(hid_chunk(z, y), mine, local_sem)
        local.start()
        local.wait()
        yield
        seq = [(0,)] + pairs
        for i, pair in enumerate(pairs):
            for k in pair:
                for copy in by_z[k]:
                    copy.wait_recv()
                zs = (z - k + NZ) % NZ
                there = H.at[core, my_rows, lanes(zs, y)]
                by_y[k] = [start(za.at[zs, j - 1], there, y_dev[j]) for j in (1, 3, 2)]
            if i + 2 < len(pairs):
                send_z(pairs[i + 2])
            yield
            finish(seq[i])
            if i:
                cross(seq[i - 1])
            yield
        finish(seq[-1])
        cross(seq[-2])
        yield
        cross(seq[-1])
        yield
        for copy in c_copies:
            copy.wait_recv()

    def shard(b, zs, ys, half=None):
        first = (zs * NY + ys) * 128
        size = 128
        if half is not None:
            first, size = first + half * 64, 64
        return C.at[b, pl.ds(pl.multiple_of(first, 64), size), :]

    def gather_task(b):
        src = cot.at[:, pl.ds(b * BCOLS, BCOLS)]
        mine = shard(b, z, y)
        right, left = start(src, mine, z_dev[1]), start(src, mine, z_dev[NZ - 1])
        pushed = [(z, start(src, mine, y_dev[1]), start(src, mine, y_dev[3]))]
        C[b, pl.ds(pl.multiple_of((z * NY + y) * 128, 128), 128), :] = cot[:, b * BCOLS : (b + 1) * BCOLS]
        last = []

        def forward():
            for zi, up, down in pushed:
                up.wait_recv()
                ref = shard(b, zi, (y + 3) % NY, 0)
                last.append(start(ref, ref, y_dev[1]))
                down.wait_recv()
                ref = shard(b, zi, (y + 1) % NY, 1)
                last.append(start(ref, ref, y_dev[3]))

        for t in range(1, 5):
            yield
            right.wait_recv()
            left.wait_recv()
            low, high = (z - t + NZ) % NZ, (z + t) % NZ
            if t < 4:
                half = (0, 1) if t == 3 else (None, None)
                ref = shard(b, low, y, half[0])
                right = start(ref, ref, z_dev[1])
                ref = shard(b, high, y, half[1])
                left = start(ref, ref, z_dev[NZ - 1])
            now = []
            for zi in (low, high) if t < 4 else (low,):
                ref = shard(b, zi, y)
                now.append((zi, start(ref, ref, y_dev[1]), start(ref, ref, y_dev[3])))
            yield
            forward()
            pushed = now
        yield
        forward()
        yield
        for copy in last:
            copy.wait_recv()

    def basis_task():
        first = pl.multiple_of(dp_of(z, xl, y) * 8, 8)
        mine = whole.at[pl.ds(first, 8), :]
        copies = [start(basis, mine, plane_dev[k]) for k in range(1, 8)]
        whole[pl.ds(first, 8), :] = basis[...]
        yield
        for copy in copies:
            copy.wait_recv()

        def level(zs, half=None):
            at, size = zs * 64, 64
            if half is not None:
                at, size = at + half * 32, 32
            return whole.at[pl.ds(pl.multiple_of(at, 32), size), :]

        right, left = start(level(z), level(z), z_dev[1]), start(level(z), level(z), z_dev[NZ - 1])
        for t in range(1, 5):
            yield
            right.wait_recv()
            left.wait_recv()
            if t < 4:
                half = (0, 1) if t == 3 else (None, None)
                ref = level((z - t + NZ) % NZ, half[0])
                right = start(ref, ref, z_dev[1])
                ref = level((z + t) % NZ, half[1])
                left = start(ref, ref, z_dev[NZ - 1])

    def product(b, rows):
        def step(kk, acc):
            k = pl.ds(pl.multiple_of(kk * DEPTH, DEPTH), DEPTH)
            return acc + jnp.dot(H[rows, :, k], C[b, k, :], preferred_element_type=jnp.float32)

        return lax.fori_loop(0, 4096 // DEPTH, step, jnp.zeros((HROWS, BCOLS), jnp.float32))

    cross = []

    def aligned(value):
        return pltpu.roll(value, (HROWS - shift) % HROWS, 0)[:ROWS]

    def columns(b):
        return slice(b * BCOLS, (b + 1) * BCOLS)

    def multiply(b):
        part[b] = product(b, 1 - xl)
        cross.append(start(part.at[b], came.at[b], xl_dev))
        turn()
        out[:ROWS, columns(b)] = mom[:, columns(b)] + aligned(product(b, xl))
        out[ROWS:, columns(b)] = jnp.zeros((PAD_ROWS - ROWS, BCOLS), jnp.float32)
        turn()

    def add(b):
        cross[b].wait_recv()
        out[:ROWS, columns(b)] += aligned(came[b])

    gathers = [gather_task(b) for b in range(BLOCKS)]
    hidden = hidden_task()
    running = [gathers[0], hidden, gathers[1]]
    waiting = [gathers[2], gathers[3]]
    for task in running:
        next(task)
    basis_gather = basis_task()

    def turn():
        for task in list(running):
            if next(task, "end") == "end":
                running.remove(task)
                if waiting and task is not hidden:
                    running.append(waiting.pop(0))


    turn()
    next(basis_gather)
    running.append(basis_gather)
    while hidden in running:
        turn()
    for b in range(BLOCKS):
        while gathers[b] in running or gathers[b] in waiting:
            turn()
        multiply(b)
        if b:
            add(b - 1)
    while running:
        turn()
    add(BLOCKS - 1)
    for copy in started:
        copy.wait_send()


PB = 16

def tdot(a, b):
    return lax.dot_general(a, b, (((0,), (0,)), ((), ())), precision=lax.Precision.HIGHEST, preferred_element_type=jnp.float32)

def eliminate(R0, R1, first):
    n = R0.shape[0]
    row_id = lax.broadcasted_iota(jnp.int32, (n, 128), 0)
    cols = [jnp.broadcast_to(R0[:, first + m : first + m + 1], (n, 128)) for m in range(n)]
    pivots = jnp.ones((n, 128), jnp.float32)
    for j in range(n):
        d = jnp.broadcast_to(cols[j][j : j + 1, :], (n, 128))
        pivots = jnp.where(row_id == j, d, pivots)
        if j + 1 < n:
            f = jnp.where(row_id > j, cols[j], 0.0) * (1.0 / d)
            for m in range(j + 1, n):
                cols[m] = cols[m] - f * cols[m][j : j + 1, :]
            R0 = R0 - f * R0[j : j + 1, :]
            R1 = R1 - f * R1[j : j + 1, :]
    scale = 1.0 / jnp.sqrt(pivots)
    return R0 * scale, R1 * scale

def factor_panel(S, work, p):
    rows = pl.ds(p * 128, 128)
    work[:, :128] = S[rows, p * 128 : p * 128 + 128]
    r = lax.broadcasted_iota(jnp.int32, (128, 128), 0)
    c = lax.broadcasted_iota(jnp.int32, (128, 128), 1)
    work[:, 128:] = jnp.where(r == c, 1.0, 0.0).astype(jnp.float32)
    for b in range(128 // PB):
        lo = b * PB
        u0, u1 = eliminate(work[lo : lo + PB, :128], work[lo : lo + PB, 128:], lo)
        work[lo : lo + PB, 128:] = u1
        if b + 1 < 128 // PB:
            u = jnp.concatenate([u0, u1], axis=1)
            upd = tdot(u0, u)
            work[lo + PB :, :] = work[lo + PB :, :] - upd[lo + PB :, :]

def panel_step(S, work, p):
    factor_panel(S, work, p)
    rows = slice(p * 128, p * 128 + 128)
    end = 512 + (p + 1) * 128
    start = p * 128
    u = jnp.dot(work[:, 128:], S[rows, start:end], precision=lax.Precision.HIGHEST, preferred_element_type=jnp.float32)
    S[rows, start:end] = u
    if p < 3:
        tr = tdot(u[:, 128 : 512 - start], u[:, 128:])
        S[(p + 1) * 128 : 512, start + 128 : end] = S[(p + 1) * 128 : 512, start + 128 : end] - tr

PAD_ROWS = 464
HALF_ROWS = PAD_ROWS // 2
HIGHEST = lax.Precision.HIGHEST


def dot_nt(a, b):
    return lax.dot_general(
        a, b, (((1,), (1,)), ((), ())), precision=HIGHEST, preferred_element_type=jnp.float32
    )


def update_kernel(
    merged, basis, ortho, right, unit,
    lpart, lcame, lown, lxcame, left, gram, gcame, gplane, gz, gsum, gfull, S, work,
    w, wsum, ay, ax, az, ay_acc, ax_acc, cx, cy, cz, cx_acc, cy_acc, sq, sqcame,
    send_sems, recv_sems,
):
    z, xl, y = place()
    mp = lax.axis_index("mp")
    core = mp % 2
    z_dev = [{"dp": dp_of((z + k) % NZ, xl, y)} for k in range(NZ)]
    y_dev = [{"dp": dp_of(z, xl, (y + k) % NY)} for k in range(NY)]
    x_dev = [None, {"dp": dp_of(z, 1 - xl, y)}]
    plane = [((xl + i) % NXL, (y + j) % NY) for i in range(NXL) for j in range(NY)]
    plane_dev = [{"dp": dp_of(z, a, b)} for a, b in plane]
    xh_dev = {"mp": (mp + 2) % 4}
    core_dev = {"mp": mp + 1 - 2 * core}
    far_dev = {"mp": (mp + 2) % 4 + 1 - 2 * core}

    count = iter(range(UPDATE_SEMS))
    started = []

    def start(src, dst, device):
        s = next(count)
        copy = send(src, dst, send_sems.at[s], recv_sems.at[s], device)
        started.append(copy)
        return copy

    def rows(first, size):
        return pl.ds(pl.multiple_of(first, 8), size)

    def left_part(half):
        there = rows(half * HALF_ROWS, HALF_ROWS)

        def step(t, _):
            cols = pl.ds(pl.multiple_of(t * 256, 256), 256)
            lpart[there, cols] = dot_nt(merged[there, :], basis[cols, :])
            return 0

        lax.fori_loop(0, 2, step, 0)

    left_part(1 - core)
    swap = start(lpart.at[rows((1 - core) * HALF_ROWS, HALF_ROWS)], lcame, core_dev)
    left_part(core)
    swap.wait_recv()
    mine = rows(core * HALF_ROWS, HALF_ROWS)
    lown[...] = lpart[mine, :] + lcame[...]
    swap = start(lown, lxcame, xh_dev)
    swap.wait_recv()
    left[mine, :] = lown[...] + lxcame[...]
    left_swap = start(left.at[mine], left.at[mine], core_dev)

    def gram_step(t, _):
        cols = pl.ds(pl.multiple_of(t * 128, 128), 128)
        gram[cols, :] = tdot(left[mine, cols], left[mine, :])
        return 0

    lax.fori_loop(0, 4, gram_step, 0)
    swap = start(gram.at[rows((1 - core) * 256, 256)], gcame, core_dev)
    swap.wait_recv()
    gcame[...] = gcame[...] + gram[rows(core * 256, 256), :]
    copies = [
        start(gcame.at[rows((a * NY + b) * 32, 32)], gplane.at[k - 1], plane_dev[k])
        for k, (a, b) in enumerate(plane)
        if k
    ]
    left_swap.wait_recv()

    def w_step(t, _):
        cols = pl.ds(pl.multiple_of(t * 128, 128), 128)
        part = tdot(merged[:, cols], left[...])
        w[0, cols, :] = part[:, :256]
        w[1, cols, :] = part[:, 256:]
        return 0

    lax.fori_loop(0, 8, w_step, 0)

    def sum_task(half, axes):
        source, first, size = w.at[half], 0, 1024
        for n, me, devices, came, acc in axes:
            size = size // n
            pieces = [
                start(source.at[rows(((me + k) % n) * size, size)], came.at[k - 1], devices[k])
                for k in range(1, n)
            ]
            yield
            total = source[rows(me * size, size), :]
            for k in range(n - 1):
                pieces[k].wait_recv()
                total = total + came[k]
            first = first + me * size
            if acc is not None:
                acc[...] = total
                source = acc
        wsum[half, rows(first, size), :] = total
        for n, me, devices, came, acc in reversed(axes):
            ref = wsum.at[half, rows(first, size)]
            pieces = [start(ref, ref, devices[k]) for k in range(1, n)]
            yield
            for copy in pieces:
                copy.wait_recv()
            first = first - me * size
            size = size * n

    y_axis, x_axis, z_axis = (NY, y, y_dev), (NXL, xl, x_dev), (NZ, z, z_dev)
    sums = [
        sum_task(0, [(*y_axis, ay, ay_acc), (*x_axis, ax, ax_acc), (*z_axis, az, None)]),
        sum_task(1, [(*x_axis, cx, cx_acc), (*y_axis, cy, cy_acc), (*z_axis, cz, None)]),
    ]

    def go_on():
        for task in list(sums):
            if next(task, "end") == "end":
                sums.remove(task)

    total = gcame[rows((xl * NY + y) * 32, 32), :]
    for k in range(7):
        copies[k].wait_recv()
        total = total + gplane[k]
    gsum[...] = total

    def z_block(ref, i):
        return ref.at[rows((i // 2) * 8, 8), pl.ds(pl.multiple_of((i % 2) * 256, 256), 256)]

    copies = [
        start(z_block(gsum, (z + k) % NZ), gz.at[k - 1], z_dev[k]) for k in range(1, NZ)
    ]
    go_on()
    my_block = z_block(gsum, z)
    total = my_block[...]
    for k in range(7):
        copies[k].wait_recv()
        total = total + gz[k]
    base = core * 256 + (xl * NY + y) * 32
    here = z_block(gfull.at[rows(base, 32)], z)
    here[...] = total
    copies = [start(here, here, z_dev[k]) for k in range(1, NZ)]
    for copy in copies:
        copy.wait_recv()
    here = gfull.at[rows(base, 32)]
    copies = [start(here, here, plane_dev[k]) for k in range(1, 8)]
    go_on()
    for copy in copies:
        copy.wait_recv()
    here = gfull.at[rows(core * 256, 256)]
    swap = start(here, here, core_dev)
    go_on()
    swap.wait_recv()

    S[:, :512] = gfull[...]
    r = lax.broadcasted_iota(jnp.int32, (512, 512), 0)
    c = lax.broadcasted_iota(jnp.int32, (512, 512), 1)
    S[:, 512:] = jnp.where(r == c, 1.0, 0.0).astype(jnp.float32)
    for p in range(4):
        panel_step(S, work, p)
        go_on()
    while sums:
        go_on()

    def right_step(t, total):
        here = pl.ds(pl.multiple_of(t * 128, 128), 128)
        both = jnp.concatenate([wsum[0, here, :], wsum[1, here, :]], axis=1)
        value = dot_nt(both, S[:, 512:])
        right[here, :] = value
        return total + jnp.sum((value * value).reshape(16, 8, 512), axis=0)

    total = lax.fori_loop(0, 8, right_step, jnp.zeros((8, 512), jnp.float32))
    sq[...] = total
    copies = [
        start(sq, sqcame.at[i], device) for i, device in enumerate([core_dev, xh_dev, far_dev])
    ]

    def ortho_step(t, _):
        here = pl.ds(pl.multiple_of(t * HALF_ROWS, 8), HALF_ROWS)
        ortho[here, :] = dot_nt(left[here, :], S[:, 512:])
        return 0

    lax.fori_loop(0, 2, ortho_step, 0)
    for copy in copies:
        copy.wait_recv()
    squares = jnp.sum(sq[...] + sqcame[0] + sqcame[1] + sqcame[2], axis=0, keepdims=True)
    unit[...] = right[...] * (1.0 / (jnp.sqrt(squares) + epsilon))
    for copy in started:
        copy.wait_send()


UPDATE_SEMS = 84


GRAD_SCRATCH = 8


def whole_kernel(hid, cot, mom, basis, merged, ortho, right, unit, whole, *scratch):
    grad_kernel(hid, cot, mom, basis, merged, whole, *scratch[:GRAD_SCRATCH])
    update_kernel(merged, whole, ortho, right, unit, *scratch[GRAD_SCRATCH:])


def merge_and_update(hidden_t, cotangent, momentum, basis):
    bf16, f32 = jnp.bfloat16, jnp.float32
    vmem = pl.BlockSpec(memory_space=pltpu.VMEM)

    def buffer(*shape):
        return pltpu.VMEM(shape, f32)

    return pl.pallas_call(
        whole_kernel,
        out_shape=(
            jax.ShapeDtypeStruct((PAD_ROWS, 1024), f32),
            jax.ShapeDtypeStruct((PAD_ROWS, RANK), f32),
            jax.ShapeDtypeStruct((1024, RANK), f32),
            jax.ShapeDtypeStruct((1024, RANK), f32),
        ),
        in_specs=[pl.BlockSpec(memory_space=pl.ANY), vmem, vmem, vmem],
        out_specs=(vmem, vmem, vmem, vmem),
        scratch_shapes=[
            buffer(RANK, 1024),
            pltpu.VMEM((2, HROWS, 4096), bf16),
            pltpu.VMEM((NZ, NY - 1, HALF, 128), bf16),
            pltpu.VMEM((BLOCKS, 4096, BCOLS), bf16),
            buffer(BLOCKS, HROWS, BCOLS),
            buffer(BLOCKS, HROWS, BCOLS),
            pltpu.SemaphoreType.DMA((N_SEMS,)),
            pltpu.SemaphoreType.DMA((N_SEMS,)),
            pltpu.SemaphoreType.DMA,
            buffer(PAD_ROWS, RANK),
            buffer(HALF_ROWS, RANK),
            buffer(HALF_ROWS, RANK),
            buffer(HALF_ROWS, RANK),
            buffer(PAD_ROWS, RANK),
            buffer(RANK, RANK),
            buffer(256, RANK),
            buffer(7, 32, RANK),
            buffer(7, 8, 256),
            buffer(32, RANK),
            buffer(RANK, RANK),
            buffer(RANK, 2 * RANK),
            buffer(128, 256),
            buffer(2, 1024, 256),
            buffer(2, 1024, 256),
            buffer(3, 256, 256),
            buffer(1, 128, 256),
            buffer(7, 16, 256),
            buffer(256, 256),
            buffer(128, 256),
            buffer(1, 512, 256),
            buffer(3, 128, 256),
            buffer(7, 16, 256),
            buffer(512, 256),
            buffer(128, 256),
            buffer(8, RANK),
            buffer(3, 8, RANK),
            pltpu.SemaphoreType.DMA((UPDATE_SEMS,)),
            pltpu.SemaphoreType.DMA((UPDATE_SEMS,)),
        ],
        compiler_params=pltpu.CompilerParams(
            collective_id=1, has_side_effects=True, vmem_limit_bytes=56 << 20
        ),
    )(hidden_t, cotangent, momentum, basis.T)


def per_device(hidden_t, cotangent, momentum, basis):
    high = lax.Precision.HIGH
    merged, orthonormal, right_full, unit_cols = merge_and_update(
        hidden_t, cotangent, momentum, basis
    )
    merged, orthonormal = merged[:ROWS], orthonormal[:ROWS]
    rank_share = basis.shape[1]
    new_basis = lax.dynamic_slice_in_dim(
        unit_cols, lax.axis_index("dp") * rank_share, rank_share, 1
    )
    new_momentum = merged - (1.0 - momentum_rate) * jnp.dot(
        orthonormal, right_full.T, precision=high
    )
    direction_scale = (FF * D / RANK) ** 0.5
    direction = (direction_scale * jnp.dot(orthonormal, unit_cols.T, precision=high)).astype(
        jnp.bfloat16
    )
    return (new_momentum, new_basis, direction)


def solution(mesh):
    in_specs = (P(None, "dp"), P("dp", "mp"), P("dp", "mp"), P("mp", "dp"))
    out_specs = (P("dp", "mp"), P("mp", "dp"), P("dp", "mp"))
    return jax.shard_map(
        per_device, mesh=mesh, in_specs=in_specs, out_specs=out_specs, check_vma=False
    )
```
